512 devices in a mesh: ctx: 128 (over z, x, y_hi), head: 4 (over y_lo, core).
Axes of the slice: x: 4, y: 4 (y_hi: 2, y_lo: 2; y = y_hi * 2 + y_lo), z: 16, core: 2. Of those that a mesh axis runs over, the one named last changes fastest.
Arguments:
- inputs: bfloat16 [65536, 4096], P('ctx', 'head'), may hold values from -6 to 6
- queries: bfloat16 [65536, 2048], P('ctx', 'head'), may hold values from -112 to 112
- keys: bfloat16 [65536, 2048], P('ctx', 'head'), may hold values from -4 to 4
- values: bfloat16 [65536, 2048], P('ctx', 'head'), may hold values from -6 to 6
- output_gradient: bfloat16 [65536, 2048], P('ctx', 'head'), may hold values from -6 to 6
- adapter_down_maps: bfloat16 [3, 4096, 16], P(None, 'head'), may hold values from -0.09375 to 0.09375
- adapter_up_maps: bfloat16 [3, 16, 2048], P(None, None, 'head'), may hold values from -0.125 to 0.125
- shifted_head_flags: int32 [16], P('head'), may hold values from 0 to 1, as said below
Outputs:
- qkv_input_gradients: bfloat16 [3, 65536, 2048], P(None, 'ctx', 'head')
- grad_down: float32 [3, 4096, 16], P(None, 'head')
- grad_up: float32 [3, 16, 2048], P(None, None, 'head')
The draws below stay inside these ranges and needn't reach their ends.
Inputs may be any that keep to these rules, and one draw needn't show every extreme that they name: `shifted_head_flags`: exactly half of the 16 heads have flag 1.
All inputs are finite; a program needn't handle non-finite values.
Results may differ from the reference program's by a relative error of at most 0.02.
Values may be sent and summed in bfloat16 or wider, within the bound.
No kernel may reach another device: no remote copies, remote signals or barrier semaphores. Data moves between devices by JAX's collectives and lax.ppermute only.
A program may use at most 64 MiB of HBM per device.

```python
import math
import jax
import jax.numpy as jnp
from jax import lax

MODEL_WIDTH = 4096
LOCAL_HEADS = 16
HEAD_SIZE = 128
ADAPTER_RANK = 16
GROUP = 1024
SHIFT = 512
TOKENS = 65536


def draw_queries(key, part):
    key = jax.random.fold_in(key, 1)
    drawn_rows = jnp.clip(jax.random.normal(key, (TOKENS, LOCAL_HEADS * HEAD_SIZE), jnp.float32), -4.0, 4.0)
    return drawn_rows.astype(jnp.bfloat16)


def draw_keys(key, part):
    key = jax.random.fold_in(key, 2)
    drawn_rows = jnp.clip(jax.random.normal(key, (TOKENS, LOCAL_HEADS * HEAD_SIZE), jnp.float32), -4.0, 4.0)
    return drawn_rows.astype(jnp.bfloat16)


def draw_shifted_head_flags(key, part):
    key = jax.random.fold_in(key, 5)
    order = jax.random.permutation(key, LOCAL_HEADS)
    return (order < LOCAL_HEADS // 2).astype(jnp.int32)


def level_of(stream_key, dims, split, smallest, high):
    def one(dim, blocks):
        heights = jax.random.uniform(jax.random.fold_in(jax.random.fold_in(stream_key, 6), dim), (blocks,), jnp.float32, smallest / len(split), high / len(split))
        return jnp.repeat(jnp.exp(heights), dims[dim] // blocks).reshape((-1,) + (1,) * (len(dims) - dim - 1))

    loudness = one(*split[0])
    for cut in split[1:]:
        loudness = loudness * one(*cut)
    return loudness


def scatter_about(stream_key, dims, scale, most, cuts=(), held_as=jnp.bfloat16):
    values = scale * jax.random.normal(stream_key, dims, jnp.float32)
    if cuts:
        values = values * level_of(stream_key, dims, cuts, -0.22, 0.18)
    return jnp.clip(values, -most, most).astype(held_as)


def setup_inputs(seed: int = 0) -> dict:
    seeds = jax.random.split(jax.random.key(seed), 9)
    inputs = scatter_about(seeds[0], (TOKENS, MODEL_WIDTH), 1.0, 6.0, ((0, 128), (1, 4)))
    queries = draw_queries(jax.random.fold_in(seeds[8], 71), 0)
    keys = draw_keys(jax.random.fold_in(seeds[8], 71), 0)
    values = scatter_about(seeds[3], (TOKENS, LOCAL_HEADS * HEAD_SIZE), 1.0, 6.0, ((0, 128), (1, 4)))
    output_gradient = scatter_about(seeds[4], (TOKENS, LOCAL_HEADS * HEAD_SIZE), 1.0, 6.0, ((0, 128), (1, 4)))
    adapter_down_maps = scatter_about(seeds[5], (3, MODEL_WIDTH, ADAPTER_RANK), MODEL_WIDTH ** -0.5, 0.09375, ((1, 4),))
    adapter_up_maps = scatter_about(seeds[6], (3, ADAPTER_RANK, LOCAL_HEADS * HEAD_SIZE), (LOCAL_HEADS * HEAD_SIZE) ** -0.5, 0.125, ((2, 4),))
    shifted_head_flags = draw_shifted_head_flags(jax.random.fold_in(seeds[8], 71), 0)
    return {"inputs": inputs, "queries": queries, "keys": keys, "values": values, "output_gradient": output_gradient, "adapter_down_maps": adapter_down_maps, "adapter_up_maps": adapter_up_maps, "shifted_head_flags": shifted_head_flags}


def head_grads(head_index, queries, keys, values, output_gradient, shifted_head_flags):
    head_flag = shifted_head_flags[head_index]

    def take_head(matrix):
        column = lax.dynamic_slice_in_dim(matrix, head_index * HEAD_SIZE, HEAD_SIZE, 1)
        column = jnp.where(head_flag == 1, jnp.roll(column, -SHIFT, 0), column)
        return column.reshape(TOKENS // GROUP, GROUP, HEAD_SIZE).astype(jnp.float32)

    def put_back(matrix):
        matrix = matrix.reshape(TOKENS, HEAD_SIZE)
        return jnp.where(head_flag == 1, jnp.roll(matrix, SHIFT, 0), matrix).astype(jnp.bfloat16)
    query_rows = take_head(queries)
    key_rows = take_head(keys)
    value_rows = take_head(values)
    grad_rows = take_head(output_gradient)
    score_scale = 1.0 / math.sqrt(HEAD_SIZE)
    causal = jnp.tril(jnp.ones((GROUP, GROUP), dtype=bool))
    scores = jnp.einsum('gqd,gkd->gqk', query_rows, key_rows) * score_scale
    scores = jnp.where(causal[None], scores, -jnp.inf)
    row_top = lax.optimization_barrier(jnp.max(scores, axis=2, keepdims=True))
    exponent = jnp.exp(scores - row_top)
    row_sum = lax.optimization_barrier(jnp.sum(exponent, axis=2, keepdims=True))
    soft_weights = exponent / row_sum
    weights_low = soft_weights.astype(jnp.bfloat16).astype(jnp.float32)
    attn_out = jnp.einsum('gqk,gkd->gqd', weights_low, value_rows)
    row_delta = lax.optimization_barrier(jnp.sum(grad_rows * attn_out, axis=2, keepdims=True))
    dprobs = jnp.einsum('gqd,gkd->gqk', grad_rows, value_rows)
    dscores = (soft_weights * (dprobs - row_delta)).astype(jnp.bfloat16).astype(jnp.float32)
    query_grad = jnp.einsum('gqk,gkd->gqd', dscores, key_rows) * score_scale
    key_grad = jnp.einsum('gqk,gqd->gkd', dscores, query_rows) * score_scale
    value_grad = jnp.einsum('gqk,gqd->gkd', weights_low, grad_rows)
    return (put_back(query_grad), put_back(key_grad), put_back(value_grad))

def reference(inputs, queries, keys, values, output_gradient, adapter_down_maps, adapter_up_maps, shifted_head_flags):

    def one_head(head_index):
        return head_grads(head_index, queries, keys, values, output_gradient, shifted_head_flags)
    per_head = lax.map(one_head, jnp.arange(LOCAL_HEADS, dtype=jnp.int32))
    qkv_input_gradients = jnp.stack([piece.transpose(1, 0, 2).reshape(TOKENS, LOCAL_HEADS * HEAD_SIZE) for piece in per_head])
    norm_factor = 1.0 / math.sqrt(TOKENS)
    down_list = []
    up_list = []
    for projection_index in range(3):
        reduced_rank_part = jnp.dot(inputs, adapter_down_maps[projection_index], preferred_element_type=jnp.float32).astype(jnp.bfloat16)
        backward_projection = jnp.dot(qkv_input_gradients[projection_index], adapter_up_maps[projection_index].T, preferred_element_type=jnp.float32).astype(jnp.bfloat16)
        down_list.append(jnp.dot(inputs.T, backward_projection, preferred_element_type=jnp.float32) * norm_factor)
        up_list.append(jnp.dot(reduced_rank_part.T, qkv_input_gradients[projection_index], preferred_element_type=jnp.float32) * norm_factor)
    return (qkv_input_gradients, jnp.stack(down_list), jnp.stack(up_list))
```

```python
import functools
import math

import jax
import jax.numpy as jnp
from jax import lax
from jax.experimental import pallas as pl
from jax.experimental.pallas import tpu as pltpu
from jax.sharding import Mesh, PartitionSpec as P

HEAD = 128
RANK = 16
TILE = 256
CTX = ("z", "x", "yh")
NEAR = ("x", "yh")
F32 = jnp.float32
BF16 = jnp.bfloat16
VMEM_BYTES = 48 * 1024 * 1024


def dot_nt(left, right):
    return lax.dot_general(left, right, (((1,), (1,)), ((), ())), preferred_element_type=F32)


def dot_tn(left, right):
    return lax.dot_general(left, right, (((0,), (0,)), ((), ())), preferred_element_type=F32)


def dot_nn(left, right):
    return lax.dot_general(left, right, (((1,), (0,)), ((), ())), preferred_element_type=F32)


def list_heads(role_ref, order_ref, wanted):
    count = jnp.int32(0)
    for head in range(role_ref.shape[0]):
        chosen = role_ref[head] == wanted

        @pl.when(chosen)
        def _():
            order_ref[count] = head

        count = count + chosen.astype(jnp.int32)
    return count


def columns_of(head):
    return pl.ds(pl.multiple_of(head * HEAD, HEAD), HEAD)


def causal_mask(rows):
    keys = lax.broadcasted_iota(jnp.int32, (rows, rows), 0)
    queries = lax.broadcasted_iota(jnp.int32, (rows, rows), 1)
    return keys <= queries


def scores_t(key_rows, query_rows, masked):
    scores = dot_nt(key_rows, query_rows)
    if masked:
        scores = jnp.where(causal_mask(TILE), scores, -jnp.inf)
    return scores


def tile_pieces(tile, own, before):
    pieces = [] if before is None else [(before, 0, before[0].shape[0], False)]
    if own is not None:
        if tile:
            pieces.append((own, 0, tile * TILE, False))
        pieces.append((own, tile * TILE, TILE, True))
    return pieces


def row_stats(pieces, query_rows, grad_rows, factor):
    scores = [
        scores_t(pair[0][start : start + rows], query_rows, masked)
        for pair, start, rows, masked in pieces
    ]
    top = functools.reduce(jnp.maximum, [jnp.max(s, axis=0, keepdims=True) for s in scores])
    total = jnp.zeros_like(top)
    mixed = jnp.zeros_like(top)
    for s, (pair, start, rows, _) in zip(scores, pieces):
        exponent = jnp.exp2((s - top) * factor)
        dprobs = dot_nt(pair[1][start : start + rows], grad_rows)
        total = total + jnp.sum(exponent, axis=0, keepdims=True)
        mixed = mixed + jnp.sum(exponent * dprobs, axis=0, keepdims=True)
    inverse = 1.0 / total
    return top, inverse, mixed * inverse


def piece_back(piece, query_rows, grad_rows, stats, factor):
    pair, start, rows, masked = piece
    top, inverse, delta = stats
    scores = scores_t(pair[0][start : start + rows], query_rows, masked)
    probs = jnp.exp2((scores - top) * factor) * inverse
    dprobs = dot_nt(pair[1][start : start + rows], grad_rows)
    dscores = (probs * (dprobs - delta)).astype(BF16)
    return probs.astype(BF16), dscores


def head_back(queries, grads, own, before, stats_of, factor, scale, want_query):
    tok_rows = queries.shape[0]
    key_grad, value_grad = {}, {}
    query_grad = []
    for tile in range(tok_rows // TILE):
        query_rows = queries[tile * TILE : (tile + 1) * TILE]
        grad_rows = grads[tile * TILE : (tile + 1) * TILE]
        stats = stats_of(tile)
        query_t = None
        for piece in tile_pieces(tile, own, before):
            pair, start, rows, masked = piece
            probs, dscores = piece_back(piece, query_rows, grad_rows, stats, factor)
            if want_query:
                term = dot_tn(pair[0][start : start + rows], dscores)
                query_t = term if query_t is None else query_t + term
            if want_query and pair is before:
                continue
            key_term = dot_nn(dscores, query_rows)
            value_term = dot_nn(probs, grad_rows)
            for part in range(rows // TILE):
                cut = slice(part * TILE, (part + 1) * TILE)
                block = start // TILE + part
                if block in key_grad:
                    key_grad[block] = key_grad[block] + key_term[cut]
                    value_grad[block] = value_grad[block] + value_term[cut]
                else:
                    key_grad[block] = key_term[cut]
                    value_grad[block] = value_term[cut]
        if want_query:
            query_grad.append(query_t.T * scale)
    blocks = range(tok_rows // TILE)
    key_grad = jnp.concatenate([key_grad[b] for b in blocks], 0) * scale
    value_grad = jnp.concatenate([value_grad[b] for b in blocks], 0)
    return (jnp.concatenate(query_grad, 0) if want_query else None), key_grad, value_grad


def pack_kernel(wanted, role_ref, a_ref, b_ref, out_ref, order_ref):
    count = list_heads(role_ref, order_ref, wanted)

    def step(slot, _):
        cols = columns_of(order_ref[slot])
        out_ref[slot, 0] = a_ref[:, cols]
        out_ref[slot, 1] = b_ref[:, cols]
        return 0

    lax.fori_loop(0, count, step, 0)


def first_kernel(factor, scale, role_ref, q_ref, k_ref, v_ref, g_ref, dq_ref, dk_ref, dv_ref, order_ref):
    count = list_heads(role_ref, order_ref, 0)

    def step(slot, _):
        cols = columns_of(order_ref[slot])
        queries, grads = q_ref[:, cols], g_ref[:, cols]
        own = (k_ref[:, cols], v_ref[:, cols])

        def stats_of(tile):
            cut = slice(tile * TILE, (tile + 1) * TILE)
            return row_stats(tile_pieces(tile, own, None), queries[cut], grads[cut], factor)

        dq, dk, dv = head_back(queries, grads, own, None, stats_of, factor, scale, True)
        dq_ref[slot] = dq.astype(BF16)
        dk_ref[slot] = dk
        dv_ref[slot] = dv
        return 0

    lax.fori_loop(0, count, step, 0)


def stats_kernel(factor, role_ref, q_ref, k_ref, v_ref, g_ref, kv_ref, stats_ref, order_ref):
    count = list_heads(role_ref, order_ref, 1)

    def step(slot, _):
        cols = columns_of(order_ref[slot])
        own = (k_ref[:, cols], v_ref[:, cols])
        before = (kv_ref[slot, 0], kv_ref[slot, 1])
        for tile in range(q_ref.shape[0] // TILE):
            cut = slice(tile * TILE, (tile + 1) * TILE)
            rows = row_stats(
                tile_pieces(tile, own, before), q_ref[cut, cols], g_ref[cut, cols], factor
            )
            for index in range(3):
                stats_ref[slot, index : index + 1, cut] = rows[index]
        return 0

    lax.fori_loop(0, count, step, 0)


def second_kernel(factor, scale, role_ref, q_ref, k_ref, v_ref, g_ref, kv_ref, stats_ref, out_ref, order_ref):
    count = list_heads(role_ref, order_ref, 1)

    def step(slot, _):
        cols = columns_of(order_ref[slot])
        own = (k_ref[:, cols], v_ref[:, cols])
        before = (kv_ref[slot, 0], kv_ref[slot, 1])

        def stats_of(tile):
            cut = slice(tile * TILE, (tile + 1) * TILE)
            return tuple(stats_ref[slot, index : index + 1, cut] for index in range(3))

        grads = head_back(
            q_ref[:, cols], g_ref[:, cols], own, before, stats_of, factor, scale, True
        )
        for index in range(3):
            out_ref[slot, index] = grads[index].astype(BF16)
        return 0

    lax.fori_loop(0, count, step, 0)


def last_kernel(
    factor, scale, role_ref, k_ref, v_ref, qg_ref, stats_ref, dq_ref, dk_ref, dv_ref, second_ref,
    up_ref, out_ref, back_ref, order_ref,
):
    count = list_heads(role_ref, order_ref, 1)

    def copy(slot, _):
        cols = columns_of(order_ref[slot])
        for index in range(3):
            out_ref[index, :, cols] = second_ref[slot, index]
        return 0

    lax.fori_loop(0, count, copy, 0)
    count = list_heads(role_ref, order_ref, 0)

    def step(slot, _):
        cols = columns_of(order_ref[slot])
        before = (k_ref[:, cols], v_ref[:, cols])

        def stats_of(tile):
            cut = slice(tile * TILE, (tile + 1) * TILE)
            return tuple(stats_ref[slot, index : index + 1, cut] for index in range(3))

        _, dk, dv = head_back(
            qg_ref[slot, 0], qg_ref[slot, 1], None, before, stats_of, factor, scale, False
        )
        out_ref[0, :, cols] = dq_ref[slot]
        out_ref[1, :, cols] = (dk_ref[slot] + dk).astype(BF16)
        out_ref[2, :, cols] = (dv_ref[slot] + dv).astype(BF16)
        return 0

    lax.fori_loop(0, count, step, 0)
    for index in range(3):
        back_ref[index * RANK : (index + 1) * RANK] = dot_nt(up_ref[index], out_ref[index]).astype(BF16)


def adapter_kernel(norm_factor, parts_ref, inputs_ref, qkv_ref, out_ref):
    summed = functools.reduce(
        jnp.add, [parts_ref[index].astype(F32) for index in range(parts_ref.shape[0])]
    ).astype(BF16)
    rows = 3 * RANK
    down = dot_nn(summed[:rows], inputs_ref[...]) * norm_factor
    up = jnp.concatenate(
        [
            dot_nn(summed[rows + index * RANK : rows + (index + 1) * RANK], qkv_ref[index])
            for index in range(3)
        ],
        0,
    ) * norm_factor
    place = 0
    for total in (down, up):
        for start in range(0, total.shape[1], HEAD):
            out_ref[place : place + rows] = total[:, start : start + HEAD].astype(BF16)
            place += rows


VMEM = pl.BlockSpec(memory_space=pltpu.VMEM)
SMEM = pl.BlockSpec(memory_space=pltpu.SMEM)


def call(kernel, outs, in_specs, flops, heads=0):
    many = isinstance(outs, (list, tuple))
    return pl.pallas_call(
        kernel,
        out_shape=outs,
        in_specs=in_specs,
        out_specs=[VMEM] * len(outs) if many else VMEM,
        scratch_shapes=[pltpu.SMEM((heads,), jnp.int32)] if heads else [],
        compiler_params=pltpu.CompilerParams(vmem_limit_bytes=VMEM_BYTES),
        cost_estimate=pl.CostEstimate(flops=flops, bytes_accessed=4 << 20, transcendentals=0),
    )


def shape(dims, dtype):
    return jax.ShapeDtypeStruct(dims, dtype)


def attention(slots, role, queries, keys, values, grads, inputs, down_t, up):
    tok_rows = queries.shape[0]
    heads = role.shape[0]
    scale = 1.0 / math.sqrt(HEAD)
    factor = scale * math.log2(math.e)
    count = lax.axis_size(CTX)
    ahead = [(source, (source + 1) % count) for source in range(count)]
    behind = [(source, (source - 1) % count) for source in range(count)]
    pair = shape((slots, 2, tok_rows, HEAD), BF16)
    low = shape((slots, tok_rows, HEAD), BF16)
    full = shape((slots, tok_rows, HEAD), F32)
    unit = 2 * tok_rows * tok_rows * HEAD * slots

    kv = call(functools.partial(pack_kernel, 0), pair, [SMEM, VMEM, VMEM], 1000, heads)(role, keys, values)
    kv = lax.ppermute(kv, CTX, ahead)
    qg = call(functools.partial(pack_kernel, 1), pair, [SMEM, VMEM, VMEM], 1000, heads)(role, queries, grads)
    qg = lax.ppermute(qg, CTX, behind)
    low_rank = dot_nt(down_t, inputs).astype(BF16)
    first = call(
        functools.partial(first_kernel, factor, scale), [low, full, full], [SMEM] + [VMEM] * 4, 6 * unit, heads
    )(role, queries, keys, values, grads)
    stats = call(
        functools.partial(stats_kernel, factor),
        shape((slots, 8, tok_rows), F32),
        [SMEM] + [VMEM] * 5,
        4 * unit,
        heads,
    )(role, queries, keys, values, grads, kv)
    moved = lax.ppermute(stats, CTX, behind)
    second = call(
        functools.partial(second_kernel, factor, scale),
        shape((slots, 3, tok_rows, HEAD), BF16),
        [SMEM] + [VMEM] * 6,
        8 * unit,
        heads,
    )(role, queries, keys, values, grads, kv, stats)
    qkv, back = call(
        functools.partial(last_kernel, factor, scale),
        [shape((3,) + queries.shape, BF16), shape((3 * RANK, tok_rows), BF16)],
        [SMEM] + [VMEM] * 9,
        4 * unit,
        heads,
    )(role, keys, values, qg, moved, *first, second, up)
    return qkv, jnp.concatenate([back, low_rank], 0)


def local(inputs, queries, keys, values, grads, down, up, flags):
    tok_rows = queries.shape[0]
    heads = flags.shape[0]
    width = inputs.shape[1]
    seq_total = lax.axis_size(CTX) * tok_rows
    role = (lax.axis_index(CTX) + flags) % 2
    shifted = jnp.sum(flags)
    slots = jnp.maximum(shifted, heads - shifted)
    least = (heads + 1) // 2
    down_t = down.transpose(0, 2, 1).reshape(3 * RANK, width)
    qkv, parts = lax.switch(
        slots - least,
        [functools.partial(attention, number) for number in range(least, heads + 1)],
        role, queries, keys, values, grads, inputs, down_t, up,
    )
    parts = lax.all_gather(parts, "head")
    rows = 3 * RANK * (width + queries.shape[1]) // HEAD
    near = lax.axis_size(NEAR)
    grad = call(
        functools.partial(adapter_kernel, 1.0 / math.sqrt(seq_total)),
        shape((rows, HEAD), BF16),
        [VMEM] * 3,
        1 << 28,
    )(parts, inputs, qkv)
    grad = lax.all_to_all(grad.reshape(near, rows // near, HEAD), NEAR, 0, 0)
    grad = jnp.sum(grad.astype(F32), 0).astype(BF16)
    far = lax.axis_size("z")
    grad = lax.all_to_all(jnp.broadcast_to(grad, (far,) + grad.shape), "z", 0, 0)
    grad = jnp.sum(grad.astype(F32), 0).astype(BF16)
    grad = lax.all_to_all(jnp.broadcast_to(grad, (near,) + grad.shape), NEAR, 0, 0)
    grad = grad.reshape(-1, 3, RANK, HEAD).astype(F32)
    split = width // HEAD
    grad_down = grad[:split].transpose(1, 0, 3, 2).reshape(3, width, RANK)
    grad_up = grad[split:].transpose(1, 2, 0, 3).reshape(3, RANK, -1)
    return qkv, grad_down, grad_up


def solution(mesh):
    count, columns = mesh.devices.shape
    across = 4 if count >= 128 else 2
    fine = Mesh(mesh.devices.reshape(count // (2 * across), across, 2, columns), CTX + ("head",))
    in_specs = (
        P(CTX, "head"),
        P(CTX, "head"),
        P(CTX, "head"),
        P(CTX, "head"),
        P(CTX, "head"),
        P(None, "head", None),
        P(None, None, "head"),
        P("head"),
    )
    out_specs = (P(None, CTX, "head"), P(None, "head", None), P(None, None, "head"))
    return jax.shard_map(local, mesh=fine, in_specs=in_specs, out_specs=out_specs, check_vma=False)
```

```python
import functools
import math

import jax
import jax.numpy as jnp
from jax import lax
from jax.experimental import pallas as pl
from jax.experimental.pallas import tpu as pltpu
from jax.sharding import Mesh, PartitionSpec as P

HEAD = 128
RANK = 16
TILE = 256
CTX = ("z", "x", "yh")
NEAR = ("x", "yh")
F32 = jnp.float32
BF16 = jnp.bfloat16
VMEM_BYTES = 48 * 1024 * 1024


def dot_nt(left, right):
    return lax.dot_general(left, right, (((1,), (1,)), ((), ())), preferred_element_type=F32)


def dot_tn(left, right):
    return lax.dot_general(left, right, (((0,), (0,)), ((), ())), preferred_element_type=F32)


def dot_nn(left, right):
    return lax.dot_general(left, right, (((1,), (0,)), ((), ())), preferred_element_type=F32)


def list_heads(role_ref, order_ref, wanted):
    count = jnp.int32(0)
    for head in range(role_ref.shape[0] - 1):
        chosen = role_ref[head] == wanted

        @pl.when(chosen)
        def _():
            order_ref[count] = head

        count = count + chosen.astype(jnp.int32)
    return count


def columns_of(head):
    return pl.ds(pl.multiple_of(head * HEAD, HEAD), HEAD)


def causal_mask(rows):
    keys = lax.broadcasted_iota(jnp.int32, (rows, rows), 0)
    queries = lax.broadcasted_iota(jnp.int32, (rows, rows), 1)
    return keys <= queries


def scores_t(key_rows, query_rows, masked):
    scores = dot_nt(key_rows, query_rows)
    if masked:
        scores = jnp.where(causal_mask(TILE), scores, -jnp.inf)
    return scores


def tile_pieces(tile, own, before):
    pieces = [] if before is None else [(before, 0, before[0].shape[0], False)]
    if own is not None:
        if tile:
            pieces.append((own, 0, tile * TILE, False))
        pieces.append((own, tile * TILE, TILE, True))
    return pieces


def row_stats(pieces, query_rows, grad_rows, factor):
    scores = [
        scores_t(pair[0][start : start + rows], query_rows, masked)
        for pair, start, rows, masked in pieces
    ]
    top = functools.reduce(jnp.maximum, [jnp.max(s, axis=0, keepdims=True) for s in scores])
    total = jnp.zeros_like(top)
    mixed = jnp.zeros_like(top)
    for s, (pair, start, rows, _) in zip(scores, pieces):
        exponent = jnp.exp2((s - top) * factor)
        dprobs = dot_nt(pair[1][start : start + rows], grad_rows)
        total = total + jnp.sum(exponent, axis=0, keepdims=True)
        mixed = mixed + jnp.sum(exponent * dprobs, axis=0, keepdims=True)
    inverse = 1.0 / total
    return top, inverse, mixed * inverse


def piece_back(piece, query_rows, grad_rows, stats, factor):
    pair, start, rows, masked = piece
    top, inverse, delta = stats
    scores = scores_t(pair[0][start : start + rows], query_rows, masked)
    probs = jnp.exp2((scores - top) * factor) * inverse
    dprobs = dot_nt(pair[1][start : start + rows], grad_rows)
    dscores = (probs * (dprobs - delta)).astype(BF16)
    return probs.astype(BF16), dscores


def head_back(queries, grads, own, before, stats_of, factor, scale, want_query):
    tok_rows = queries.shape[0]
    key_grad, value_grad = {}, {}
    query_grad = []
    for tile in range(tok_rows // TILE):
        query_rows = queries[tile * TILE : (tile + 1) * TILE]
        grad_rows = grads[tile * TILE : (tile + 1) * TILE]
        stats = stats_of(tile)
        query_t = None
        for piece in tile_pieces(tile, own, before):
            pair, start, rows, masked = piece
            probs, dscores = piece_back(piece, query_rows, grad_rows, stats, factor)
            if want_query:
                term = dot_tn(pair[0][start : start + rows], dscores)
                query_t = term if query_t is None else query_t + term
            if want_query and pair is before:
                continue
            key_term = dot_nn(dscores, query_rows)
            value_term = dot_nn(probs, grad_rows)
            for part in range(rows // TILE):
                cut = slice(part * TILE, (part + 1) * TILE)
                block = start // TILE + part
                if block in key_grad:
                    key_grad[block] = key_grad[block] + key_term[cut]
                    value_grad[block] = value_grad[block] + value_term[cut]
                else:
                    key_grad[block] = key_term[cut]
                    value_grad[block] = value_term[cut]
        if want_query:
            query_grad.append(query_t.T * scale)
    blocks = range(tok_rows // TILE)
    key_grad = jnp.concatenate([key_grad[b] for b in blocks], 0) * scale
    value_grad = jnp.concatenate([value_grad[b] for b in blocks], 0)
    return (jnp.concatenate(query_grad, 0) if want_query else None), key_grad, value_grad


def run_sides(role_ref, sides, step):
    for parity, ref, count in sides:
        if parity is None:
            lax.fori_loop(0, count, functools.partial(step, ref), 0)
        else:

            @pl.when(role_ref[role_ref.shape[0] - 1] == parity)
            def _():
                lax.fori_loop(0, count, functools.partial(step, ref), 0)


def pack_kernel(wanted, role_ref, a_ref, b_ref, out_ref, order_ref):
    list_heads(role_ref, order_ref, wanted)

    def step(slot, _):
        cols = columns_of(order_ref[slot])
        out_ref[slot, 0] = a_ref[:, cols]
        out_ref[slot, 1] = b_ref[:, cols]
        return 0

    lax.fori_loop(0, out_ref.shape[0], step, 0)


def pack_pairs_kernel(flags, role_ref, q_ref, k_ref, v_ref, g_ref, *refs):
    *out_refs, order_ref = refs
    for wanted, sent in ((0, (k_ref, v_ref)), (1, (q_ref, g_ref))):
        list_heads(role_ref, order_ref, wanted)

        def step(out_ref, slot, _):
            cols = columns_of(order_ref[slot])
            out_ref[slot, 0] = sent[0][:, cols]
            out_ref[slot, 1] = sent[1][:, cols]
            return 0

        sides = [((wanted + flag) % 2, ref, ref.shape[0]) for flag, ref in zip(flags, out_refs)]
        run_sides(role_ref, sides, step)


def first_kernel(factor, scale, role_ref, q_ref, k_ref, v_ref, g_ref, dq_ref, dk_ref, dv_ref, order_ref):
    count = list_heads(role_ref, order_ref, 0)

    def step(slot, _):
        cols = columns_of(order_ref[slot])
        queries, grads = q_ref[:, cols], g_ref[:, cols]
        own = (k_ref[:, cols], v_ref[:, cols])

        def stats_of(tile):
            cut = slice(tile * TILE, (tile + 1) * TILE)
            return row_stats(tile_pieces(tile, own, None), queries[cut], grads[cut], factor)

        dq, dk, dv = head_back(queries, grads, own, None, stats_of, factor, scale, True)
        dq_ref[slot] = dq.astype(BF16)
        dk_ref[slot] = dk
        dv_ref[slot] = dv
        return 0

    lax.fori_loop(0, count, step, 0)


def side_refs(refs, parities):
    return [(parity, ref, ref.shape[0]) for parity, ref in zip(parities, refs)]


def stats_kernel(factor, parities, role_ref, q_ref, k_ref, v_ref, g_ref, *refs):
    *kv_refs, stats_ref, order_ref = refs
    list_heads(role_ref, order_ref, 1)

    def step(kv_ref, slot, _):
        cols = columns_of(order_ref[slot])
        own = (k_ref[:, cols], v_ref[:, cols])
        before = (kv_ref[slot, 0], kv_ref[slot, 1])
        for tile in range(q_ref.shape[0] // TILE):
            cut = slice(tile * TILE, (tile + 1) * TILE)
            rows = row_stats(
                tile_pieces(tile, own, before), q_ref[cut, cols], g_ref[cut, cols], factor
            )
            for index in range(3):
                stats_ref[slot, index : index + 1, cut] = rows[index]
        return 0

    run_sides(role_ref, side_refs(kv_refs, parities), step)


def second_kernel(factor, scale, parities, role_ref, q_ref, k_ref, v_ref, g_ref, stats_ref, *refs):
    *kv_refs, out_ref, order_ref = refs
    list_heads(role_ref, order_ref, 1)

    def step(kv_ref, slot, _):
        cols = columns_of(order_ref[slot])
        own = (k_ref[:, cols], v_ref[:, cols])
        before = (kv_ref[slot, 0], kv_ref[slot, 1])

        def stats_of(tile):
            cut = slice(tile * TILE, (tile + 1) * TILE)
            return tuple(stats_ref[slot, index : index + 1, cut] for index in range(3))

        grads = head_back(
            q_ref[:, cols], g_ref[:, cols], own, before, stats_of, factor, scale, True
        )
        for index in range(3):
            out_ref[slot, index] = grads[index].astype(BF16)
        return 0

    run_sides(role_ref, side_refs(kv_refs, parities), step)


def last_kernel(
    factor, scale, parities, role_ref, k_ref, v_ref, stats_ref, dq_ref, dk_ref, dv_ref, second_ref,
    up_ref, *refs
):
    *qg_refs, out_ref, back_ref, order_ref = refs
    count = list_heads(role_ref, order_ref, 1)

    def copy(slot, _):
        cols = columns_of(order_ref[slot])
        for index in range(3):
            out_ref[index, :, cols] = second_ref[slot, index]
        return 0

    lax.fori_loop(0, count, copy, 0)
    list_heads(role_ref, order_ref, 0)

    def step(qg_ref, slot, _):
        cols = columns_of(order_ref[slot])
        before = (k_ref[:, cols], v_ref[:, cols])

        def stats_of(tile):
            cut = slice(tile * TILE, (tile + 1) * TILE)
            return tuple(stats_ref[slot, index : index + 1, cut] for index in range(3))

        _, dk, dv = head_back(
            qg_ref[slot, 0], qg_ref[slot, 1], None, before, stats_of, factor, scale, False
        )
        out_ref[0, :, cols] = dq_ref[slot]
        out_ref[1, :, cols] = (dk_ref[slot] + dk).astype(BF16)
        out_ref[2, :, cols] = (dv_ref[slot] + dv).astype(BF16)
        return 0

    run_sides(role_ref, side_refs(qg_refs, parities), step)
    for index in range(3):
        back_ref[index * RANK : (index + 1) * RANK] = dot_nt(up_ref[index], out_ref[index]).astype(BF16)


def adapter_kernel(norm_factor, parts_ref, inputs_ref, qkv_ref, out_ref):
    summed = functools.reduce(
        jnp.add, [parts_ref[index].astype(F32) for index in range(parts_ref.shape[0])]
    ).astype(BF16)
    rows = 3 * RANK
    down = dot_nn(summed[:rows], inputs_ref[...]) * norm_factor
    up = jnp.concatenate(
        [
            dot_nn(summed[rows + index * RANK : rows + (index + 1) * RANK], qkv_ref[index])
            for index in range(3)
        ],
        0,
    ) * norm_factor
    place = 0
    for total in (down, up):
        for start in range(0, total.shape[1], HEAD):
            out_ref[place : place + rows] = total[:, start : start + HEAD].astype(BF16)
            place += rows


VMEM = pl.BlockSpec(memory_space=pltpu.VMEM)
SMEM = pl.BlockSpec(memory_space=pltpu.SMEM)


def call(kernel, outs, in_specs, flops, heads=0):
    many = isinstance(outs, (list, tuple))
    return pl.pallas_call(
        kernel,
        out_shape=outs,
        in_specs=in_specs,
        out_specs=[VMEM] * len(outs) if many else VMEM,
        scratch_shapes=[pltpu.SMEM((heads,), jnp.int32)] if heads else [],
        compiler_params=pltpu.CompilerParams(vmem_limit_bytes=VMEM_BYTES),
        cost_estimate=pl.CostEstimate(flops=flops, bytes_accessed=4 << 20, transcendentals=0),
    )


def shape(dims, dtype):
    return jax.ShapeDtypeStruct(dims, dtype)


def ring(count, parity, step):
    return [(source, (source + step) % count) for source in range(parity, count, 2)]


def attention(shifted, role, queries, keys, values, grads, inputs, down_t, up):
    tok_rows = queries.shape[0]
    heads = role.shape[0] - 1
    plain = heads - shifted
    slots = max(plain, shifted)
    scale = 1.0 / math.sqrt(HEAD)
    factor = scale * math.log2(math.e)
    count = lax.axis_size(CTX)
    ahead = ring(count, 0, 1) + ring(count, 1, 1)
    behind = ring(count, 0, -1) + ring(count, 1, -1)
    low = shape((slots, tok_rows, HEAD), BF16)
    full = shape((slots, tok_rows, HEAD), F32)
    unit = 2 * tok_rows * tok_rows * HEAD * slots

    def pair(number):
        return shape((number, 2, tok_rows, HEAD), BF16)

    if plain == shifted:
        pack = [SMEM, VMEM, VMEM]
        kv = call(functools.partial(pack_kernel, 0), pair(slots), pack, 1000, heads)(role, keys, values)
        kv = [lax.ppermute(kv, CTX, ahead)]
        qg = call(functools.partial(pack_kernel, 1), pair(slots), pack, 1000, heads)(role, queries, grads)
        qg = [lax.ppermute(qg, CTX, behind)]
        kv_parities = qg_parities = [None]
    else:
        numbers = (plain, shifted)
        flags = [flag for flag in range(2) if numbers[flag]]
        packed = call(
            functools.partial(pack_pairs_kernel, flags),
            [pair(numbers[flag]) for flag in flags],
            [SMEM] + [VMEM] * 4,
            1000,
            heads,
        )(role, queries, keys, values, grads)
        moved = dict(zip(flags, packed))
        for flag in sorted(flags, key=lambda flag: -numbers[flag]):
            swap = ring(count, flag, 1) + ring(count, (flag + 1) % 2, -1)
            moved[flag] = lax.ppermute(moved[flag], CTX, swap)
        kv = qg = [moved[flag] for flag in flags]
        kv_parities = [(flag + 1) % 2 for flag in flags]
        qg_parities = flags
    low_rank = dot_nt(down_t, inputs).astype(BF16)
    first = call(
        functools.partial(first_kernel, factor, scale), [low, full, full], [SMEM] + [VMEM] * 4, 6 * unit, heads
    )(role, queries, keys, values, grads)
    stats = call(
        functools.partial(stats_kernel, factor, kv_parities),
        shape((slots, 8, tok_rows), F32),
        [SMEM] + [VMEM] * (4 + len(kv)),
        4 * unit,
        heads,
    )(role, queries, keys, values, grads, *kv)
    moved = lax.ppermute(stats, CTX, behind)
    second = call(
        functools.partial(second_kernel, factor, scale, kv_parities),
        shape((slots, 3, tok_rows, HEAD), BF16),
        [SMEM] + [VMEM] * (5 + len(kv)),
        8 * unit,
        heads,
    )(role, queries, keys, values, grads, stats, *kv)
    qkv, back = call(
        functools.partial(last_kernel, factor, scale, qg_parities),
        [shape((3,) + queries.shape, BF16), shape((3 * RANK, tok_rows), BF16)],
        [SMEM] + [VMEM] * (8 + len(qg)),
        4 * unit,
        heads,
    )(role, keys, values, moved, *first, second, up, *qg)
    return qkv, jnp.concatenate([back, low_rank], 0)


def local(inputs, queries, keys, values, grads, down, up, flags):
    tok_rows = queries.shape[0]
    heads = flags.shape[0]
    width = inputs.shape[1]
    seq_total = lax.axis_size(CTX) * tok_rows
    place = lax.axis_index(CTX)
    role = (place + jnp.concatenate([flags, jnp.zeros((1,), jnp.int32)])) & 1
    down_t = down.transpose(0, 2, 1).reshape(3 * RANK, width)
    qkv, parts = lax.switch(
        jnp.sum(flags),
        [functools.partial(attention, number) for number in range(heads + 1)],
        role, queries, keys, values, grads, inputs, down_t, up,
    )
    parts = lax.all_gather(parts, "head")
    rows = 3 * RANK * (width + queries.shape[1]) // HEAD
    near = lax.axis_size(NEAR)
    grad = call(
        functools.partial(adapter_kernel, 1.0 / math.sqrt(seq_total)),
        shape((rows, HEAD), BF16),
        [VMEM] * 3,
        1 << 28,
    )(parts, inputs, qkv)
    grad = lax.all_to_all(grad.reshape(near, rows // near, HEAD), NEAR, 0, 0)
    grad = jnp.sum(grad.astype(F32), 0).astype(BF16)
    far = lax.axis_size("z")
    grad = lax.all_to_all(jnp.broadcast_to(grad, (far,) + grad.shape), "z", 0, 0)
    grad = jnp.sum(grad.astype(F32), 0).astype(BF16)
    grad = lax.all_to_all(jnp.broadcast_to(grad, (near,) + grad.shape), NEAR, 0, 0)
    grad = grad.reshape(-1, 3, RANK, HEAD).astype(F32)
    split = width // HEAD
    grad_down = grad[:split].transpose(1, 0, 3, 2).reshape(3, width, RANK)
    grad_up = grad[split:].transpose(1, 2, 0, 3).reshape(3, RANK, -1)
    return qkv, grad_down, grad_up


def solution(mesh):
    count, columns = mesh.devices.shape
    across = 4 if count >= 128 else 2
    fine = Mesh(mesh.devices.reshape(count // (2 * across), across, 2, columns), CTX + ("head",))
    in_specs = (
        P(CTX, "head"),
        P(CTX, "head"),
        P(CTX, "head"),
        P(CTX, "head"),
        P(CTX, "head"),
        P(None, "head", None),
        P(None, None, "head"),
        P("head"),
    )
    out_specs = (P(None, CTX, "head"), P(None, "head", None), P(None, None, "head"))
    return jax.shard_map(local, mesh=fine, in_specs=in_specs, out_specs=out_specs, check_vma=False)
```

```python
import functools
import math

import jax
import jax.numpy as jnp
from jax import lax
from jax.experimental import pallas as pl
from jax.experimental.pallas import tpu as pltpu
from jax.sharding import Mesh, PartitionSpec as P

HEAD = 128
RANK = 16
TILE = 256
CTX = ("zh", "zl", "x", "yh")
FAR = "zh"
NEAR = ("zl", "x", "yh")
F32 = jnp.float32
BF16 = jnp.bfloat16
VMEM_BYTES = 48 * 1024 * 1024


def dot_nt(left, right):
    return lax.dot_general(left, right, (((1,), (1,)), ((), ())), preferred_element_type=F32)


def dot_tn(left, right):
    return lax.dot_general(left, right, (((0,), (0,)), ((), ())), preferred_element_type=F32)


def dot_nn(left, right):
    return lax.dot_general(left, right, (((1,), (0,)), ((), ())), preferred_element_type=F32)


def list_heads(role_ref, order_ref, wanted):
    count = jnp.int32(0)
    for head in range(role_ref.shape[0] - 1):
        chosen = role_ref[head] == wanted

        @pl.when(chosen)
        def _():
            order_ref[count] = head

        count = count + chosen.astype(jnp.int32)
    return count


def columns_of(head):
    return pl.ds(pl.multiple_of(head * HEAD, HEAD), HEAD)


def causal_mask(rows):
    keys = lax.broadcasted_iota(jnp.int32, (rows, rows), 0)
    queries = lax.broadcasted_iota(jnp.int32, (rows, rows), 1)
    return keys <= queries


def scores_t(key_rows, query_rows, masked):
    scores = dot_nt(key_rows, query_rows)
    if masked:
        scores = jnp.where(causal_mask(TILE), scores, -jnp.inf)
    return scores


def tile_pieces(tile, own, before):
    pieces = [] if before is None else [(before, 0, before[0].shape[0], False)]
    if own is not None:
        if tile:
            pieces.append((own, 0, tile * TILE, False))
        pieces.append((own, tile * TILE, TILE, True))
    return pieces


def row_stats(pieces, query_rows, grad_rows, factor):
    scores = [
        scores_t(pair[0][start : start + rows], query_rows, masked)
        for pair, start, rows, masked in pieces
    ]
    top = functools.reduce(jnp.maximum, [jnp.max(s, axis=0, keepdims=True) for s in scores])
    total = jnp.zeros_like(top)
    mixed = jnp.zeros_like(top)
    for s, (pair, start, rows, _) in zip(scores, pieces):
        exponent = jnp.exp2((s - top) * factor)
        dprobs = dot_nt(pair[1][start : start + rows], grad_rows)
        total = total + jnp.sum(exponent, axis=0, keepdims=True)
        mixed = mixed + jnp.sum(exponent * dprobs, axis=0, keepdims=True)
    inverse = 1.0 / total
    return top, inverse, mixed * inverse


def piece_back(piece, query_rows, grad_rows, stats, factor):
    pair, start, rows, masked = piece
    top, inverse, delta = stats
    scores = scores_t(pair[0][start : start + rows], query_rows, masked)
    probs = jnp.exp2((scores - top) * factor) * inverse
    dprobs = dot_nt(pair[1][start : start + rows], grad_rows)
    dscores = (probs * (dprobs - delta)).astype(BF16)
    return probs.astype(BF16), dscores


def head_back(queries, grads, own, before, stats_of, factor, scale, want_query):
    tok_rows = queries.shape[0]
    key_grad, value_grad = {}, {}
    query_grad = []
    for tile in range(tok_rows // TILE):
        query_rows = queries[tile * TILE : (tile + 1) * TILE]
        grad_rows = grads[tile * TILE : (tile + 1) * TILE]
        stats = stats_of(tile)
        query_t = None
        for piece in tile_pieces(tile, own, before):
            pair, start, rows, masked = piece
            probs, dscores = piece_back(piece, query_rows, grad_rows, stats, factor)
            if want_query:
                term = dot_tn(pair[0][start : start + rows], dscores)
                query_t = term if query_t is None else query_t + term
            if want_query and pair is before:
                continue
            key_term = dot_nn(dscores, query_rows)
            value_term = dot_nn(probs, grad_rows)
            for part in range(rows // TILE):
                cut = slice(part * TILE, (part + 1) * TILE)
                block = start // TILE + part
                if block in key_grad:
                    key_grad[block] = key_grad[block] + key_term[cut]
                    value_grad[block] = value_grad[block] + value_term[cut]
                else:
                    key_grad[block] = key_term[cut]
                    value_grad[block] = value_term[cut]
        if want_query:
            query_grad.append(query_t.T * scale)
    blocks = range(tok_rows // TILE)
    key_grad = jnp.concatenate([key_grad[b] for b in blocks], 0) * scale
    value_grad = jnp.concatenate([value_grad[b] for b in blocks], 0)
    return (jnp.concatenate(query_grad, 0) if want_query else None), key_grad, value_grad


def run_sides(role_ref, sides, step):
    for parity, ref, count in sides:
        if parity is None:
            lax.fori_loop(0, count, functools.partial(step, ref), 0)
        else:

            @pl.when(role_ref[role_ref.shape[0] - 1] == parity)
            def _():
                lax.fori_loop(0, count, functools.partial(step, ref), 0)


def pack_kernel(plans, role_ref, q_ref, k_ref, v_ref, g_ref, *refs):
    *out_refs, order_ref = refs
    for wanted, sent in ((0, (k_ref, v_ref)), (1, (q_ref, g_ref))):
        chosen = [(ref, plan[1]) for ref, plan in zip(out_refs, plans) if plan[0] in (wanted, None)]
        if not chosen:
            continue
        list_heads(role_ref, order_ref, wanted)

        def step(out_ref, slot, _):
            cols = columns_of(order_ref[slot])
            out_ref[slot, 0] = sent[0][:, cols]
            out_ref[slot, 1] = sent[1][:, cols]
            return 0

        sides = []
        for ref, parity in chosen:
            swapped = parity is not None and wanted == 1
            sides.append(((parity + 1) % 2 if swapped else parity, ref, ref.shape[0]))
        run_sides(role_ref, sides, step)


def first_kernel(factor, scale, role_ref, q_ref, k_ref, v_ref, g_ref, dq_ref, dk_ref, dv_ref, order_ref):
    count = list_heads(role_ref, order_ref, 0)

    def step(slot, _):
        cols = columns_of(order_ref[slot])
        queries, grads = q_ref[:, cols], g_ref[:, cols]
        own = (k_ref[:, cols], v_ref[:, cols])

        def stats_of(tile):
            cut = slice(tile * TILE, (tile + 1) * TILE)
            return row_stats(tile_pieces(tile, own, None), queries[cut], grads[cut], factor)

        dq, dk, dv = head_back(queries, grads, own, None, stats_of, factor, scale, True)
        dq_ref[slot] = dq.astype(BF16)
        dk_ref[slot] = dk
        dv_ref[slot] = dv
        return 0

    lax.fori_loop(0, count, step, 0)


def side_refs(refs, parities):
    return [(parity, ref, ref.shape[0]) for parity, ref in zip(parities, refs)]


def stats_kernel(factor, parities, role_ref, q_ref, k_ref, v_ref, g_ref, *refs):
    *kv_refs, stats_ref, order_ref = refs
    list_heads(role_ref, order_ref, 1)

    def step(kv_ref, slot, _):
        cols = columns_of(order_ref[slot])
        own = (k_ref[:, cols], v_ref[:, cols])
        before = (kv_ref[slot, 0], kv_ref[slot, 1])
        for tile in range(q_ref.shape[0] // TILE):
            cut = slice(tile * TILE, (tile + 1) * TILE)
            rows = row_stats(
                tile_pieces(tile, own, before), q_ref[cut, cols], g_ref[cut, cols], factor
            )
            for index in range(3):
                stats_ref[slot, index : index + 1, cut] = rows[index]
        return 0

    run_sides(role_ref, side_refs(kv_refs, parities), step)


def second_kernel(factor, scale, parities, role_ref, q_ref, k_ref, v_ref, g_ref, stats_ref, *refs):
    *kv_refs, out_ref, order_ref = refs
    list_heads(role_ref, order_ref, 1)

    def step(kv_ref, slot, _):
        cols = columns_of(order_ref[slot])
        own = (k_ref[:, cols], v_ref[:, cols])
        before = (kv_ref[slot, 0], kv_ref[slot, 1])

        def stats_of(tile):
            cut = slice(tile * TILE, (tile + 1) * TILE)
            return tuple(stats_ref[slot, index : index + 1, cut] for index in range(3))

        grads = head_back(
            q_ref[:, cols], g_ref[:, cols], own, before, stats_of, factor, scale, True
        )
        for index in range(3):
            out_ref[slot, index] = grads[index].astype(BF16)
        return 0

    run_sides(role_ref, side_refs(kv_refs, parities), step)


def last_kernel(
    factor, scale, parities, role_ref, k_ref, v_ref, stats_ref, dq_ref, dk_ref, dv_ref, second_ref,
    up_ref, *refs
):
    *qg_refs, out_ref, back_ref, order_ref = refs
    count = list_heads(role_ref, order_ref, 1)

    def copy(slot, _):
        cols = columns_of(order_ref[slot])
        for index in range(3):
            out_ref[index, :, cols] = second_ref[slot, index]
        return 0

    lax.fori_loop(0, count, copy, 0)
    list_heads(role_ref, order_ref, 0)

    def step(qg_ref, slot, _):
        cols = columns_of(order_ref[slot])
        before = (k_ref[:, cols], v_ref[:, cols])

        def stats_of(tile):
            cut = slice(tile * TILE, (tile + 1) * TILE)
            return tuple(stats_ref[slot, index : index + 1, cut] for index in range(3))

        _, dk, dv = head_back(
            qg_ref[slot, 0], qg_ref[slot, 1], None, before, stats_of, factor, scale, False
        )
        out_ref[0, :, cols] = dq_ref[slot]
        out_ref[1, :, cols] = (dk_ref[slot] + dk).astype(BF16)
        out_ref[2, :, cols] = (dv_ref[slot] + dv).astype(BF16)
        return 0

    run_sides(role_ref, side_refs(qg_refs, parities), step)
    for index in range(3):
        back_ref[index * RANK : (index + 1) * RANK] = dot_nt(up_ref[index], out_ref[index]).astype(BF16)


def adapter_kernel(norm_factor, parts_ref, inputs_ref, qkv_ref, out_ref):
    summed = functools.reduce(
        jnp.add, [parts_ref[index].astype(F32) for index in range(parts_ref.shape[0])]
    ).astype(BF16)
    rows = 3 * RANK
    down = dot_nn(summed[:rows], inputs_ref[...]) * norm_factor
    up = jnp.concatenate(
        [
            dot_nn(summed[rows + index * RANK : rows + (index + 1) * RANK], qkv_ref[index])
            for index in range(3)
        ],
        0,
    ) * norm_factor
    place = 0
    for total in (down, up):
        for start in range(0, total.shape[1], HEAD):
            out_ref[place : place + rows] = total[:, start : start + HEAD].astype(BF16)
            place += rows


VMEM = pl.BlockSpec(memory_space=pltpu.VMEM)
SMEM = pl.BlockSpec(memory_space=pltpu.SMEM)


def call(kernel, outs, in_specs, flops, heads=0):
    many = isinstance(outs, (list, tuple))
    return pl.pallas_call(
        kernel,
        out_shape=outs,
        in_specs=in_specs,
        out_specs=[VMEM] * len(outs) if many else VMEM,
        scratch_shapes=[pltpu.SMEM((heads,), jnp.int32)] if heads else [],
        compiler_params=pltpu.CompilerParams(vmem_limit_bytes=VMEM_BYTES),
        cost_estimate=pl.CostEstimate(flops=flops, bytes_accessed=4 << 20, transcendentals=0),
    )


def shape(dims, dtype):
    return jax.ShapeDtypeStruct(dims, dtype)


def ring(count, parity, step):
    return [(source, (source + step) % count) for source in range(parity, count, 2)]


def attention(shifted, role, queries, keys, values, grads, inputs, down_t, up):
    tok_rows = queries.shape[0]
    heads = role.shape[0] - 1
    plain = heads - shifted
    slots = max(plain, shifted)
    scale = 1.0 / math.sqrt(HEAD)
    factor = scale * math.log2(math.e)
    count = lax.axis_size(CTX)
    ahead = ring(count, 0, 1) + ring(count, 1, 1)
    behind = ring(count, 0, -1) + ring(count, 1, -1)
    low = shape((slots, tok_rows, HEAD), BF16)
    full = shape((slots, tok_rows, HEAD), F32)
    unit = 2 * tok_rows * tok_rows * HEAD * slots

    def pair(number):
        return shape((number, 2, tok_rows, HEAD), BF16)

    def packed(plans, numbers):
        return call(
            functools.partial(pack_kernel, plans),
            [pair(number) for number in numbers],
            [SMEM] + [VMEM] * 4,
            1000,
            heads,
        )(role, queries, keys, values, grads)

    def after(value, other):
        return lax.optimization_barrier((value, other))[0]

    def first_halves():
        return call(
            functools.partial(first_kernel, factor, scale), [low, full, full], [SMEM] + [VMEM] * 4, 6 * unit, heads
        )(role, queries, keys, values, grads)

    numbers = (plain, shifted)
    flags = [flag for flag in range(2) if numbers[flag]]
    if len(flags) == 1:
        flag = flags[0]
        swap = ring(count, flag, 1) + ring(count, (flag + 1) % 2, -1)
        sent = packed([(None, flag)], [heads])[0]
        kv = qg = [lax.ppermute(sent, CTX, swap)]
        first = first_halves()
        kv_parities, qg_parities = [(flag + 1) % 2], [flag]
    elif plain == shifted:
        sent = packed([(0, None), (1, None)], numbers)
        kv = [lax.ppermute(sent[0], CTX, ahead)]
        first = first_halves()
        qg = [lax.ppermute(after(sent[1], first[0]), CTX, behind)]
        kv_parities = qg_parities = [None]
    else:
        flags = sorted(flags, key=lambda flag: -numbers[flag])
        sizes = [numbers[flag] for flag in flags]
        sent = packed([(role_, flag) for role_ in range(2) for flag in flags], sizes * 2)
        kv = [lax.ppermute(sent[at], CTX, ring(count, flag, 1)) for at, flag in enumerate(flags)]
        first = first_halves()
        late = lax.optimization_barrier((sent[2], sent[3], first[0]))
        qg = [
            lax.ppermute(late[at], CTX, ring(count, (flag + 1) % 2, -1))
            for at, flag in enumerate(flags)
        ]
        kv_parities = [(flag + 1) % 2 for flag in flags]
        qg_parities = flags
    low_rank = dot_nt(down_t, inputs).astype(BF16)
    stats = call(
        functools.partial(stats_kernel, factor, kv_parities),
        shape((slots, 8, tok_rows), F32),
        [SMEM] + [VMEM] * (4 + len(kv)),
        4 * unit,
        heads,
    )(role, queries, keys, values, grads, *kv)
    moved = lax.ppermute(stats, CTX, behind)
    second = call(
        functools.partial(second_kernel, factor, scale, kv_parities),
        shape((slots, 3, tok_rows, HEAD), BF16),
        [SMEM] + [VMEM] * (5 + len(kv)),
        8 * unit,
        heads,
    )(role, queries, keys, values, grads, stats, *kv)
    qkv, back = call(
        functools.partial(last_kernel, factor, scale, qg_parities),
        [shape((3,) + queries.shape, BF16), shape((3 * RANK, tok_rows), BF16)],
        [SMEM] + [VMEM] * (8 + len(qg)),
        4 * unit,
        heads,
    )(role, keys, values, moved, *first, second, up, *qg)
    return qkv, jnp.concatenate([back, low_rank], 0)


def local(inputs, queries, keys, values, grads, down, up, flags):
    tok_rows = queries.shape[0]
    heads = flags.shape[0]
    width = inputs.shape[1]
    seq_total = lax.axis_size(CTX) * tok_rows
    place = lax.axis_index(CTX)
    role = (place + jnp.concatenate([flags, jnp.zeros((1,), jnp.int32)])) & 1
    down_t = down.transpose(0, 2, 1).reshape(3 * RANK, width)
    qkv, parts = lax.switch(
        jnp.sum(flags),
        [functools.partial(attention, number) for number in range(heads + 1)],
        role, queries, keys, values, grads, inputs, down_t, up,
    )
    parts = lax.all_gather(parts, "head")
    rows = 3 * RANK * (width + queries.shape[1]) // HEAD
    grad = call(
        functools.partial(adapter_kernel, 1.0 / math.sqrt(seq_total)),
        shape((rows, HEAD), BF16),
        [VMEM] * 3,
        1 << 28,
    )(parts, inputs, qkv)
    near = lax.axis_size(NEAR)
    grad = lax.all_to_all(grad.reshape(near, rows // near, HEAD), NEAR, 0, 0)
    grad = jnp.sum(grad.astype(F32), 0).astype(BF16)
    far = lax.axis_size(FAR)
    grad = lax.all_to_all(jnp.broadcast_to(grad, (far,) + grad.shape), FAR, 0, 0)
    grad = jnp.sum(grad.astype(F32), 0).astype(BF16)
    grad = lax.all_to_all(jnp.broadcast_to(grad, (near,) + grad.shape), NEAR, 0, 0)
    grad = grad.reshape(-1, 3, RANK, HEAD).astype(F32)
    split = width // HEAD
    grad_down = grad[:split].transpose(1, 0, 3, 2).reshape(3, width, RANK)
    grad_up = grad[split:].transpose(1, 2, 0, 3).reshape(3, RANK, -1)
    return qkv, grad_down, grad_up


def solution(mesh):
    count, columns = mesh.devices.shape
    across = 4 if count >= 128 else 2
    fine = Mesh(mesh.devices.reshape(-1, 2, across, 2, columns), CTX + ("head",))
    in_specs = (
        P(CTX, "head"),
        P(CTX, "head"),
        P(CTX, "head"),
        P(CTX, "head"),
        P(CTX, "head"),
        P(None, "head", None),
        P(None, None, "head"),
        P("head"),
    )
    out_specs = (P(None, CTX, "head"), P(None, "head", None), P(None, None, "head"))
    return jax.shard_map(local, mesh=fine, in_specs=in_specs, out_specs=out_specs, check_vma=False)
```

```python
import functools
import math

import jax
import jax.numpy as jnp
from jax import lax
from jax.experimental import pallas as pl
from jax.experimental.pallas import tpu as pltpu
from jax.sharding import Mesh, PartitionSpec as P

HEAD = 128
RANK = 16
TILE = 256
CTX = ("zh", "zl", "x", "yh")
FAR = "zh"
NEAR = ("zl", "x", "yh")
F32 = jnp.float32
BF16 = jnp.bfloat16
VMEM_BYTES = 48 * 1024 * 1024


def dot_nt(left, right):
    return lax.dot_general(left, right, (((1,), (1,)), ((), ())), preferred_element_type=F32)


def dot_tn(left, right):
    return lax.dot_general(left, right, (((0,), (0,)), ((), ())), preferred_element_type=F32)


def dot_nn(left, right):
    return lax.dot_general(left, right, (((1,), (0,)), ((), ())), preferred_element_type=F32)


def list_heads(role_ref, order_ref, wanted):
    count = jnp.int32(0)
    for head in range(role_ref.shape[0] - 1):
        chosen = role_ref[head] == wanted

        @pl.when(chosen)
        def _():
            order_ref[count] = head

        count = count + chosen.astype(jnp.int32)
    return count


def columns_of(head):
    return pl.ds(pl.multiple_of(head * HEAD, HEAD), HEAD)


def causal_mask(rows):
    keys = lax.broadcasted_iota(jnp.int32, (rows, rows), 0)
    queries = lax.broadcasted_iota(jnp.int32, (rows, rows), 1)
    return keys <= queries


def row_stats(scores, dprobs, factor):
    top = functools.reduce(jnp.maximum, [jnp.max(s, axis=0, keepdims=True) for s in scores])
    exponents = [jnp.exp2((s - top) * factor) for s in scores]
    total = sum(jnp.sum(e, axis=0, keepdims=True) for e in exponents)
    mixed = sum(jnp.sum(e * d, axis=0, keepdims=True) for e, d in zip(exponents, dprobs))
    return exponents, (top, total, mixed)


def merge_stats(one, other, factor):
    top = jnp.maximum(one[0], other[0])
    weights = [jnp.exp2((stats[0] - top) * factor) for stats in (one, other)]
    total = one[1] * weights[0] + other[1] * weights[1]
    mixed = one[2] * weights[0] + other[2] * weights[1]
    return top, total, mixed


def low_parts(probs, dprobs, delta):
    return probs.astype(BF16), (probs * (dprobs - delta)).astype(BF16)


class Tile:
    def __init__(self, queries, grads, index, factor):
        cut = slice(index * TILE, (index + 1) * TILE)
        self.queries, self.grads = queries[cut], grads[cut]
        self.index, self.factor = index, factor

    def products(self, pair, start, rows, masked):
        scores = dot_nt(pair[0][start : start + rows], self.queries)
        if masked:
            scores = jnp.where(causal_mask(TILE), scores, -jnp.inf)
        return scores, dot_nt(pair[1][start : start + rows], self.grads)

    def own_pieces(self):
        before = [(0, self.index * TILE, False)] if self.index else []
        return before + [(self.index * TILE, TILE, True)]

    def own_stats(self, own):
        products = [self.products(own, *piece) for piece in self.own_pieces()]
        exponents, stats = row_stats(*zip(*products), self.factor)
        return exponents, [dprobs for _, dprobs in products], stats

    def full_block(self, pair, own_stats):
        scores, dprobs = self.products(pair, 0, pair[0].shape[0], False)
        (exponent,), stats = row_stats([scores], [dprobs], self.factor)
        top, total, mixed = merge_stats(stats, own_stats, self.factor)
        inverse = 1.0 / total
        delta = mixed * inverse
        probs = exponent * (jnp.exp2((stats[0] - top) * self.factor) * inverse)
        return low_parts(probs, dprobs, delta), (top, inverse, delta)


class Sums:
    def __init__(self):
        self.parts = {}

    def add(self, start, value):
        for at in range(0, value.shape[0], TILE):
            part = value[at : at + TILE]
            held = self.parts.get(start + at)
            self.parts[start + at] = part if held is None else held + part

    def whole(self):
        return jnp.concatenate([self.parts[at] for at in sorted(self.parts)], 0)


def plan_kernel(flags_ref, role_ref, shifted_ref):
    parity = lax.axis_index("yh")
    total = jnp.int32(0)
    for head in range(flags_ref.shape[0]):
        role_ref[head] = (flags_ref[head] + parity) & 1
        total = total + flags_ref[head]
    role_ref[flags_ref.shape[0]] = parity
    shifted_ref[0] = total


def run_sides(role_ref, sides, step):
    for parity, ref, count in sides:
        if parity is None:
            lax.fori_loop(0, count, functools.partial(step, ref), 0)
        else:

            @pl.when(role_ref[role_ref.shape[0] - 1] == parity)
            def _():
                lax.fori_loop(0, count, functools.partial(step, ref), 0)


def pack_kernel(plans, role_ref, q_ref, k_ref, v_ref, g_ref, *refs):
    *out_refs, order_ref = refs
    for wanted, sent in ((0, (k_ref, v_ref)), (1, (q_ref, g_ref))):
        chosen = [(ref, plan[1]) for ref, plan in zip(out_refs, plans) if plan[0] in (wanted, None)]
        if not chosen:
            continue
        list_heads(role_ref, order_ref, wanted)

        def step(out_ref, slot, _):
            cols = columns_of(order_ref[slot])
            out_ref[slot, 0] = sent[0][:, cols]
            out_ref[slot, 1] = sent[1][:, cols]
            return 0

        sides = []
        for ref, parity in chosen:
            swapped = parity is not None and wanted == 1
            sides.append(((parity + 1) % 2 if swapped else parity, ref, ref.shape[0]))
        run_sides(role_ref, sides, step)


def early_kernel(factor, scale, role_ref, q_ref, k_ref, v_ref, g_ref, dq_ref, dk_ref, dv_ref, stats_ref, order_ref):
    tiles = range(q_ref.shape[0] // TILE)
    count = list_heads(role_ref, order_ref, 1)

    def rows(slot, _):
        cols = columns_of(order_ref[slot])
        own = (k_ref[:, cols], v_ref[:, cols])
        for index in tiles:
            tile = Tile(q_ref[:, cols], g_ref[:, cols], index, factor)
            _, _, stats = tile.own_stats(own)
            for row in range(3):
                stats_ref[slot, row : row + 1, index * TILE : (index + 1) * TILE] = stats[row]
        return 0

    lax.fori_loop(0, count, rows, 0)
    count = list_heads(role_ref, order_ref, 0)

    def step(slot, _):
        cols = columns_of(order_ref[slot])
        own = (k_ref[:, cols], v_ref[:, cols])
        key_sums, value_sums = Sums(), Sums()
        for index in tiles:
            tile = Tile(q_ref[:, cols], g_ref[:, cols], index, factor)
            exponents, dprobs, (_, total, mixed) = tile.own_stats(own)
            inverse = 1.0 / total
            query_t = 0.0
            for (start, length, _), e, d in zip(tile.own_pieces(), exponents, dprobs):
                probs, dscores = low_parts(e * inverse, d, mixed * inverse)
                query_t = query_t + dot_tn(own[0][start : start + length], dscores)
                key_sums.add(start, dot_nn(dscores, tile.queries))
                value_sums.add(start, dot_nn(probs, tile.grads))
            dq_ref[slot, index * TILE : (index + 1) * TILE] = (query_t.T * scale).astype(BF16)
        dk_ref[slot] = key_sums.whole()
        dv_ref[slot] = value_sums.whole()
        return 0

    lax.fori_loop(0, count, step, 0)


def side_refs(refs, parities):
    return [(parity, ref, ref.shape[0]) for parity, ref in zip(parities, refs)]


def tile_stats(stats_ref, slot, index):
    return tuple(
        stats_ref[slot, row : row + 1, index * TILE : (index + 1) * TILE] for row in range(3)
    )


def late_kernel(
    factor, scale, kv_parities, qg_parities, role_ref, q_ref, k_ref, v_ref, g_ref, stats_ref,
    moved_ref, dq_ref, dk_ref, dv_ref, up_ref, *refs
):
    *other_refs, out_ref, back_ref, order_ref = refs
    kv_refs, qg_refs = other_refs[: len(kv_parities)], other_refs[-len(qg_parities) :]
    tiles = range(q_ref.shape[0] // TILE)
    list_heads(role_ref, order_ref, 1)

    def second(kv_ref, slot, _):
        cols = columns_of(order_ref[slot])
        own = (k_ref[:, cols], v_ref[:, cols])
        before = (kv_ref[slot, 0], kv_ref[slot, 1])
        key_sums, value_sums = Sums(), Sums()
        for index in tiles:
            tile = Tile(q_ref[:, cols], g_ref[:, cols], index, factor)
            (_, dscores), (top, inverse, delta) = tile.full_block(
                before, tile_stats(stats_ref, slot, index)
            )
            query_t = dot_tn(before[0], dscores)
            for piece in tile.own_pieces():
                start, length, _ = piece
                scores, dprobs = tile.products(own, *piece)
                probs, dscores = low_parts(
                    jnp.exp2((scores - top) * factor) * inverse, dprobs, delta
                )
                query_t = query_t + dot_tn(own[0][start : start + length], dscores)
                key_sums.add(start, dot_nn(dscores, tile.queries))
                value_sums.add(start, dot_nn(probs, tile.grads))
            out_ref[0, index * TILE : (index + 1) * TILE, cols] = (query_t.T * scale).astype(BF16)
        out_ref[1, :, cols] = (key_sums.whole() * scale).astype(BF16)
        out_ref[2, :, cols] = value_sums.whole().astype(BF16)
        return 0

    run_sides(role_ref, side_refs(kv_refs, kv_parities), second)
    list_heads(role_ref, order_ref, 0)

    def first(qg_ref, slot, _):
        cols = columns_of(order_ref[slot])
        own = (k_ref[:, cols], v_ref[:, cols])
        dk, dv = dk_ref[slot], dv_ref[slot]
        for index in tiles:
            tile = Tile(qg_ref[slot, 0], qg_ref[slot, 1], index, factor)
            (probs, dscores), _ = tile.full_block(own, tile_stats(moved_ref, slot, index))
            dk = dk + dot_nn(dscores, tile.queries)
            dv = dv + dot_nn(probs, tile.grads)
        out_ref[0, :, cols] = dq_ref[slot]
        out_ref[1, :, cols] = (dk * scale).astype(BF16)
        out_ref[2, :, cols] = dv.astype(BF16)
        return 0

    run_sides(role_ref, side_refs(qg_refs, qg_parities), first)
    for index in range(3):
        back_ref[index * RANK : (index + 1) * RANK] = dot_nt(up_ref[index], out_ref[index]).astype(BF16)


def adapter_kernel(norm_factor, parts_ref, inputs_ref, qkv_ref, out_ref):
    summed = functools.reduce(
        jnp.add, [parts_ref[index].astype(F32) for index in range(parts_ref.shape[0])]
    ).astype(BF16)
    rows = 3 * RANK
    down = dot_nn(summed[:rows], inputs_ref[...]) * norm_factor
    up = jnp.concatenate(
        [
            dot_nn(summed[rows + index * RANK : rows + (index + 1) * RANK], qkv_ref[index])
            for index in range(3)
        ],
        0,
    ) * norm_factor
    place = 0
    for total in (down, up):
        for start in range(0, total.shape[1], HEAD):
            out_ref[place : place + rows] = total[:, start : start + HEAD].astype(BF16)
            place += rows


def finish_kernel(sums_ref, *out_refs):
    place = 0
    for out_ref in out_refs:
        for start in range(0, out_ref.shape[1], HEAD):
            rows = out_ref.shape[0]
            out_ref[:, start : start + HEAD] = sums_ref[place : place + rows].astype(F32)
            place += rows


VMEM = pl.BlockSpec(memory_space=pltpu.VMEM)
SMEM = pl.BlockSpec(memory_space=pltpu.SMEM)


def call(kernel, outs, in_specs, flops, heads=0):
    many = isinstance(outs, (list, tuple))
    return pl.pallas_call(
        kernel,
        out_shape=outs,
        in_specs=in_specs,
        out_specs=[VMEM] * len(outs) if many else VMEM,
        scratch_shapes=[pltpu.SMEM((heads,), jnp.int32)] if heads else [],
        compiler_params=pltpu.CompilerParams(vmem_limit_bytes=VMEM_BYTES),
        cost_estimate=pl.CostEstimate(flops=flops, bytes_accessed=flops >> 8, transcendentals=0),
    )


def shape(dims, dtype):
    return jax.ShapeDtypeStruct(dims, dtype)


def ring(count, parity, step):
    return [(source, (source + step) % count) for source in range(parity, count, 2)]


def attention(shifted, role, queries, keys, values, grads, inputs, down_t, up):
    tok_rows = queries.shape[0]
    heads = role.shape[0] - 1
    plain = heads - shifted
    slots = max(plain, shifted)
    scale = 1.0 / math.sqrt(HEAD)
    factor = scale * math.log2(math.e)
    count = lax.axis_size(CTX)
    ahead = ring(count, 0, 1) + ring(count, 1, 1)
    behind = ring(count, 0, -1) + ring(count, 1, -1)
    low = shape((slots, tok_rows, HEAD), BF16)
    full = shape((slots, tok_rows, HEAD), F32)
    unit = 2 * tok_rows * tok_rows * HEAD * slots

    def pair(number):
        return shape((number, 2, tok_rows, HEAD), BF16)

    def packed(plans, numbers):
        return call(
            functools.partial(pack_kernel, plans),
            [pair(number) for number in numbers],
            [SMEM] + [VMEM] * 4,
            1000,
            heads,
        )(role, queries, keys, values, grads)

    *first, stats = call(
        functools.partial(early_kernel, factor, scale),
        [low, full, full, shape((slots, 8, tok_rows), F32)],
        [SMEM] + [VMEM] * 4,
        1,
        heads,
    )(role, queries, keys, values, grads)

    stats, moved = lax.optimization_barrier((stats, lax.ppermute(stats, CTX, behind)))

    numbers = (plain, shifted)
    flags = [flag for flag in range(2) if numbers[flag]]
    if plain == shifted:
        sent = packed([(0, None)], [slots])[0]
        kv = [lax.ppermute(sent, CTX, ahead)]
        sent = packed([(1, None)], [slots])[0]
        qg = [lax.ppermute(sent, CTX, behind)]
        kv_parities = qg_parities = [None]
    else:
        flags = sorted(flags, key=lambda flag: -numbers[flag])
        sent = packed([(None, flag) for flag in flags], [numbers[flag] for flag in flags])
        kv = qg = [
            lax.ppermute(sent[at], CTX, ring(count, flag, 1) + ring(count, (flag + 1) % 2, -1))
            for at, flag in enumerate(flags)
        ]
        kv_parities = [(flag + 1) % 2 for flag in flags]
        qg_parities = flags
    low_rank = dot_nt(down_t, inputs).astype(BF16)
    arrived = kv if kv is qg else kv + qg
    qkv, back = call(
        functools.partial(late_kernel, factor, scale, kv_parities, qg_parities),
        [shape((3,) + queries.shape, BF16), shape((3 * RANK, tok_rows), BF16)],
        [SMEM] + [VMEM] * (10 + len(arrived)),
        12 * unit,
        heads,
    )(role, queries, keys, values, grads, stats, moved, *first, up, *arrived)
    return qkv, jnp.concatenate([back, low_rank], 0)


def local(inputs, queries, keys, values, grads, down, up, flags):
    tok_rows = queries.shape[0]
    heads = flags.shape[0]
    width = inputs.shape[1]
    seq_total = lax.axis_size(CTX) * tok_rows
    role, shifted = pl.pallas_call(
        plan_kernel,
        out_shape=[shape((heads + 1,), jnp.int32), shape((1,), jnp.int32)],
        in_specs=[SMEM],
        out_specs=[SMEM, SMEM],
    )(flags)
    down_t = down.transpose(0, 2, 1).reshape(3 * RANK, width)
    qkv, parts = lax.switch(
        shifted.reshape(()),
        [functools.partial(attention, number) for number in range(heads + 1)],
        role, queries, keys, values, grads, inputs, down_t, up,
    )
    parts = lax.all_gather(parts, "head")
    rows = 3 * RANK * (width + queries.shape[1]) // HEAD
    grad = call(
        functools.partial(adapter_kernel, 1.0 / math.sqrt(seq_total)),
        shape((rows, HEAD), BF16),
        [VMEM] * 3,
        1 << 28,
    )(parts, inputs, qkv)
    near = lax.axis_size(NEAR)
    grad = lax.all_to_all(grad.reshape(near, rows // near, HEAD), NEAR, 0, 0)
    grad = jnp.sum(grad.astype(F32), 0).astype(BF16)
    far = lax.axis_size(FAR)
    grad = lax.all_to_all(jnp.broadcast_to(grad, (far,) + grad.shape), FAR, 0, 0)
    grad = jnp.sum(grad.astype(F32), 0).astype(BF16)
    grad = lax.all_to_all(jnp.broadcast_to(grad, (near,) + grad.shape), NEAR, 0, 0)
    grad_down, grad_up = call(
        finish_kernel,
        [shape((3 * RANK, width), F32), shape((3 * RANK, queries.shape[1]), F32)],
        [VMEM],
        1,
    )(grad.reshape(rows, HEAD))
    grad_down = grad_down.reshape(3, RANK, width).transpose(0, 2, 1)
    grad_up = grad_up.reshape(3, RANK, -1)
    return qkv, grad_down, grad_up


def solution(mesh):
    count, columns = mesh.devices.shape
    across = 4 if count >= 128 else 2
    fine = Mesh(mesh.devices.reshape(-1, 2, across, 2, columns), CTX + ("head",))
    in_specs = (
        P(CTX, "head"),
        P(CTX, "head"),
        P(CTX, "head"),
        P(CTX, "head"),
        P(CTX, "head"),
        P(None, "head", None),
        P(None, None, "head"),
        P("head"),
    )
    out_specs = (P(None, CTX, "head"), P(None, "head", None), P(None, None, "head"))
    return jax.shard_map(local, mesh=fine, in_specs=in_specs, out_specs=out_specs, check_vma=False)
```

```python
import functools
import math

import jax
import jax.numpy as jnp
from jax import lax
from jax.experimental import pallas as pl
from jax.experimental.pallas import tpu as pltpu
from jax.sharding import Mesh, PartitionSpec as P

HEAD = 128
RANK = 16
TILE = 256
CTX = ("zh", "zl", "x", "yh")
FAR = "zh"
NEAR = ("zl", "x", "yh")
F32 = jnp.float32
BF16 = jnp.bfloat16
VMEM_BYTES = 48 * 1024 * 1024


def dot_nt(left, right):
    return lax.dot_general(left, right, (((1,), (1,)), ((), ())), preferred_element_type=F32)


def dot_tn(left, right):
    return lax.dot_general(left, right, (((0,), (0,)), ((), ())), preferred_element_type=F32)


def dot_nn(left, right):
    return lax.dot_general(left, right, (((1,), (0,)), ((), ())), preferred_element_type=F32)


def list_heads(role_ref, order_ref, wanted):
    count = jnp.int32(0)
    for head in range(role_ref.shape[0] - 1):
        chosen = role_ref[head] == wanted

        @pl.when(chosen)
        def _():
            order_ref[count] = head

        count = count + chosen.astype(jnp.int32)
    return count


def columns_of(head):
    return pl.ds(pl.multiple_of(head * HEAD, HEAD), HEAD)


def causal_mask(rows, columns):
    keys = lax.broadcasted_iota(jnp.int32, (rows, columns), 0)
    queries = lax.broadcasted_iota(jnp.int32, (rows, columns), 1)
    return keys <= queries


def merge_stats(one, other, factor):
    top = jnp.maximum(one[0], other[0])
    weights = [jnp.exp2((stats[0] - top) * factor) for stats in (one, other)]
    total = one[1] * weights[0] + other[1] * weights[1]
    mixed = one[2] * weights[0] + other[2] * weights[1]
    return top, total, mixed


def low_parts(probs, dprobs, delta):
    return probs.astype(BF16), (probs * (dprobs - delta)).astype(BF16)


def join(function, wide, narrow):
    if wide is None or wide.shape == narrow.shape:
        return narrow if wide is None else function(wide, narrow)
    first = wide.shape[1] - narrow.shape[1]
    return jnp.concatenate([wide[:, :first], function(wide[:, first:], narrow)], 1)


def col_sum(value):
    return jnp.sum(value, axis=0, keepdims=True)


class Head:
    def __init__(self, queries, grads, factor):
        self.queries, self.grads, self.factor = queries, grads, factor

    def full_block(self, pair, own_stats):
        scores = dot_nt(pair[0], self.queries)
        dprobs = dot_nt(pair[1], self.grads)
        own_top = jnp.max(scores, axis=0, keepdims=True)
        exponent = jnp.exp2((scores - own_top) * self.factor)
        stats = own_top, col_sum(exponent), col_sum(exponent * dprobs)
        top, total, mixed = merge_stats(stats, own_stats, self.factor)
        inverse = 1.0 / total
        delta = mixed * inverse
        probs = exponent * (jnp.exp2((own_top - top) * self.factor) * inverse)
        return low_parts(probs, dprobs, delta), (top, inverse, delta)

    def own_products(self, own):
        pieces = []
        for start in range(0, self.queries.shape[0], TILE):
            scores = dot_nt(own[0][start : start + TILE], self.queries[start:])
            scores = jnp.where(causal_mask(*scores.shape), scores, -jnp.inf)
            dprobs = dot_nt(own[1][start : start + TILE], self.grads[start:])
            pieces.append((start, scores, dprobs))
        return pieces

    def own_stats(self, pieces):
        top = total = mixed = None
        for _, scores, _ in pieces:
            top = join(jnp.maximum, top, jnp.max(scores, axis=0, keepdims=True))
        exponents = []
        for start, scores, dprobs in pieces:
            exponents.append(jnp.exp2((scores - top[:, start:]) * self.factor))
            total = join(jnp.add, total, col_sum(exponents[-1]))
            mixed = join(jnp.add, mixed, col_sum(exponents[-1] * dprobs))
        return exponents, (top, total, mixed)

    def own_block(self, own, weights):
        query_t, key_grads, value_grads = None, [], []
        for start, probs, dprobs, delta in weights:
            probs, dscores = low_parts(probs, dprobs, delta)
            query_t = join(jnp.add, query_t, dot_tn(own[0][start : start + TILE], dscores))
            key_grads.append(dot_nn(dscores, self.queries[start:]))
            value_grads.append(dot_nn(probs, self.grads[start:]))
        return query_t, jnp.concatenate(key_grads, 0), jnp.concatenate(value_grads, 0)


def plan_kernel(flags_ref, role_ref, shifted_ref):
    parity = lax.axis_index("yh")
    total = jnp.int32(0)
    for head in range(flags_ref.shape[0]):
        role_ref[head] = (flags_ref[head] + parity) & 1
        total = total + flags_ref[head]
    role_ref[flags_ref.shape[0]] = parity
    shifted_ref[0] = total


def run_sides(role_ref, sides, step):
    for parity, ref, count in sides:
        if parity is None:
            lax.fori_loop(0, count, functools.partial(step, ref), 0)
        else:

            @pl.when(role_ref[role_ref.shape[0] - 1] == parity)
            def _():
                lax.fori_loop(0, count, functools.partial(step, ref), 0)


def pack_kernel(plans, role_ref, q_ref, k_ref, v_ref, g_ref, *refs):
    *out_refs, order_ref = refs
    for wanted, sent in ((0, (k_ref, v_ref)), (1, (q_ref, g_ref))):
        chosen = [(ref, plan[1]) for ref, plan in zip(out_refs, plans) if plan[0] in (wanted, None)]
        if not chosen:
            continue
        list_heads(role_ref, order_ref, wanted)

        def step(out_ref, slot, _):
            cols = columns_of(order_ref[slot])
            out_ref[slot, 0] = sent[0][:, cols]
            out_ref[slot, 1] = sent[1][:, cols]
            return 0

        sides = []
        for ref, parity in chosen:
            swapped = parity is not None and wanted == 1
            sides.append(((parity + 1) % 2 if swapped else parity, ref, ref.shape[0]))
        run_sides(role_ref, sides, step)


def early_kernel(factor, scale, role_ref, q_ref, k_ref, v_ref, g_ref, dq_ref, dk_ref, dv_ref, stats_ref, order_ref):
    count = list_heads(role_ref, order_ref, 1)

    def rows(slot, _):
        cols = columns_of(order_ref[slot])
        head = Head(q_ref[:, cols], g_ref[:, cols], factor)
        _, stats = head.own_stats(head.own_products((k_ref[:, cols], v_ref[:, cols])))
        for row in range(3):
            stats_ref[slot, row : row + 1] = stats[row]
        return 0

    lax.fori_loop(0, count, rows, 0)
    count = list_heads(role_ref, order_ref, 0)

    def step(slot, _):
        cols = columns_of(order_ref[slot])
        own = (k_ref[:, cols], v_ref[:, cols])
        head = Head(q_ref[:, cols], g_ref[:, cols], factor)
        pieces = head.own_products(own)
        exponents, (_, total, mixed) = head.own_stats(pieces)
        inverse = 1.0 / total
        delta = mixed * inverse
        query_t, dk, dv = head.own_block(
            own,
            [
                (start, exponent * inverse[:, start:], dprobs, delta[:, start:])
                for (start, _, dprobs), exponent in zip(pieces, exponents)
            ],
        )
        dq_ref[slot] = (query_t.T * scale).astype(BF16)
        dk_ref[slot] = dk
        dv_ref[slot] = dv
        return 0

    lax.fori_loop(0, count, step, 0)


def side_refs(refs, parities):
    return [(parity, ref, ref.shape[0]) for parity, ref in zip(parities, refs)]


def head_stats(stats_ref, slot):
    return tuple(stats_ref[slot, row : row + 1] for row in range(3))


def late_kernel(
    factor, scale, kv_parities, qg_parities, role_ref, q_ref, k_ref, v_ref, g_ref, stats_ref,
    moved_ref, dq_ref, dk_ref, dv_ref, up_ref, *refs
):
    *other_refs, out_ref, back_ref, order_ref = refs
    kv_refs, qg_refs = other_refs[: len(kv_parities)], other_refs[-len(qg_parities) :]
    list_heads(role_ref, order_ref, 1)

    def second(kv_ref, slot, _):
        cols = columns_of(order_ref[slot])
        own = (k_ref[:, cols], v_ref[:, cols])
        before = (kv_ref[slot, 0], kv_ref[slot, 1])
        head = Head(q_ref[:, cols], g_ref[:, cols], factor)
        (_, dscores), (top, inverse, delta) = head.full_block(before, head_stats(stats_ref, slot))
        query_t, dk, dv = head.own_block(
            own,
            [
                (
                    start,
                    jnp.exp2((scores - top[:, start:]) * factor) * inverse[:, start:],
                    dprobs,
                    delta[:, start:],
                )
                for start, scores, dprobs in head.own_products(own)
            ],
        )
        query_t = query_t + dot_tn(before[0], dscores)
        out_ref[0, :, cols] = (query_t.T * scale).astype(BF16)
        out_ref[1, :, cols] = (dk * scale).astype(BF16)
        out_ref[2, :, cols] = dv.astype(BF16)
        return 0

    run_sides(role_ref, side_refs(kv_refs, kv_parities), second)
    list_heads(role_ref, order_ref, 0)

    def first(qg_ref, slot, _):
        cols = columns_of(order_ref[slot])
        head = Head(qg_ref[slot, 0], qg_ref[slot, 1], factor)
        (probs, dscores), _ = head.full_block(
            (k_ref[:, cols], v_ref[:, cols]), head_stats(moved_ref, slot)
        )
        out_ref[0, :, cols] = dq_ref[slot]
        out_ref[1, :, cols] = ((dk_ref[slot] + dot_nn(dscores, head.queries)) * scale).astype(BF16)
        out_ref[2, :, cols] = (dv_ref[slot] + dot_nn(probs, head.grads)).astype(BF16)
        return 0

    run_sides(role_ref, side_refs(qg_refs, qg_parities), first)
    for index in range(3):
        back_ref[index * RANK : (index + 1) * RANK] = dot_nt(up_ref[index], out_ref[index]).astype(BF16)


def adapter_kernel(norm_factor, parts_ref, inputs_ref, qkv_ref, out_ref):
    summed = functools.reduce(
        jnp.add, [parts_ref[index].astype(F32) for index in range(parts_ref.shape[0])]
    ).astype(BF16)
    rows = 3 * RANK
    down = dot_nn(summed[:rows], inputs_ref[...]) * norm_factor
    up = jnp.concatenate(
        [
            dot_nn(summed[rows + index * RANK : rows + (index + 1) * RANK], qkv_ref[index])
            for index in range(3)
        ],
        0,
    ) * norm_factor
    place = 0
    for total in (down, up):
        for start in range(0, total.shape[1], HEAD):
            out_ref[place : place + rows] = total[:, start : start + HEAD].astype(BF16)
            place += rows


def finish_kernel(sums_ref, *out_refs):
    place = 0
    for out_ref in out_refs:
        for start in range(0, out_ref.shape[1], HEAD):
            rows = out_ref.shape[0]
            out_ref[:, start : start + HEAD] = sums_ref[place : place + rows].astype(F32)
            place += rows


VMEM = pl.BlockSpec(memory_space=pltpu.VMEM)
SMEM = pl.BlockSpec(memory_space=pltpu.SMEM)


def call(kernel, outs, in_specs, flops, heads=0):
    many = isinstance(outs, (list, tuple))
    return pl.pallas_call(
        kernel,
        out_shape=outs,
        in_specs=in_specs,
        out_specs=[VMEM] * len(outs) if many else VMEM,
        scratch_shapes=[pltpu.SMEM((heads,), jnp.int32)] if heads else [],
        compiler_params=pltpu.CompilerParams(vmem_limit_bytes=VMEM_BYTES),
        cost_estimate=pl.CostEstimate(flops=flops, bytes_accessed=flops >> 8, transcendentals=0),
    )


def shape(dims, dtype):
    return jax.ShapeDtypeStruct(dims, dtype)


def ring(count, parity, step):
    return [(source, (source + step) % count) for source in range(parity, count, 2)]


def attention(shifted, role, queries, keys, values, grads, inputs, down_t, up):
    tok_rows = queries.shape[0]
    heads = role.shape[0] - 1
    plain = heads - shifted
    slots = max(plain, shifted)
    scale = 1.0 / math.sqrt(HEAD)
    factor = scale * math.log2(math.e)
    count = lax.axis_size(CTX)
    ahead = ring(count, 0, 1) + ring(count, 1, 1)
    behind = ring(count, 0, -1) + ring(count, 1, -1)
    low = shape((slots, tok_rows, HEAD), BF16)
    full = shape((slots, tok_rows, HEAD), F32)
    unit = 2 * tok_rows * tok_rows * HEAD * slots

    def pair(number):
        return shape((number, 2, tok_rows, HEAD), BF16)

    def packed(plans, numbers):
        return call(
            functools.partial(pack_kernel, plans),
            [pair(number) for number in numbers],
            [SMEM] + [VMEM] * 4,
            1000,
            heads,
        )(role, queries, keys, values, grads)

    *first, stats = call(
        functools.partial(early_kernel, factor, scale),
        [low, full, full, shape((slots, 8, tok_rows), F32)],
        [SMEM] + [VMEM] * 4,
        1,
        heads,
    )(role, queries, keys, values, grads)

    stats, moved = lax.optimization_barrier((stats, lax.ppermute(stats, CTX, behind)))

    numbers = (plain, shifted)
    flags = [flag for flag in range(2) if numbers[flag]]
    if plain == shifted:
        sent = packed([(0, None)], [slots])[0]
        kv = [lax.ppermute(sent, CTX, ahead)]
        sent = packed([(1, None)], [slots])[0]
        qg = [lax.ppermute(sent, CTX, behind)]
        kv_parities = qg_parities = [None]
    else:
        flags = sorted(flags, key=lambda flag: -numbers[flag])
        sent = packed([(None, flag) for flag in flags], [numbers[flag] for flag in flags])
        kv = qg = [
            lax.ppermute(sent[at], CTX, ring(count, flag, 1) + ring(count, (flag + 1) % 2, -1))
            for at, flag in enumerate(flags)
        ]
        kv_parities = [(flag + 1) % 2 for flag in flags]
        qg_parities = flags
    low_rank = dot_nt(down_t, inputs).astype(BF16)
    arrived = kv if kv is qg else kv + qg
    qkv, back = call(
        functools.partial(late_kernel, factor, scale, kv_parities, qg_parities),
        [shape((3,) + queries.shape, BF16), shape((3 * RANK, tok_rows), BF16)],
        [SMEM] + [VMEM] * (10 + len(arrived)),
        12 * unit,
        heads,
    )(role, queries, keys, values, grads, stats, moved, *first, up, *arrived)
    return qkv, jnp.concatenate([back, low_rank], 0)


def local(inputs, queries, keys, values, grads, down, up, flags):
    tok_rows = queries.shape[0]
    heads = flags.shape[0]
    width = inputs.shape[1]
    seq_total = lax.axis_size(CTX) * tok_rows
    role, shifted = pl.pallas_call(
        plan_kernel,
        out_shape=[shape((heads + 1,), jnp.int32), shape((1,), jnp.int32)],
        in_specs=[SMEM],
        out_specs=[SMEM, SMEM],
    )(flags)
    down_t = down.transpose(0, 2, 1).reshape(3 * RANK, width)
    qkv, parts = lax.switch(
        shifted.reshape(()),
        [functools.partial(attention, number) for number in range(heads + 1)],
        role, queries, keys, values, grads, inputs, down_t, up,
    )
    parts = lax.all_gather(parts, "head")
    rows = 3 * RANK * (width + queries.shape[1]) // HEAD
    grad = call(
        functools.partial(adapter_kernel, 1.0 / math.sqrt(seq_total)),
        shape((rows, HEAD), BF16),
        [VMEM] * 3,
        1 << 28,
    )(parts, inputs, qkv)
    near = lax.axis_size(NEAR)
    grad = lax.all_to_all(grad.reshape(near, rows // near, HEAD), NEAR, 0, 0)
    grad = jnp.sum(grad.astype(F32), 0).astype(BF16)
    far = lax.axis_size(FAR)
    grad = lax.all_to_all(jnp.broadcast_to(grad, (far,) + grad.shape), FAR, 0, 0)
    grad = jnp.sum(grad.astype(F32), 0).astype(BF16)
    grad = lax.all_to_all(jnp.broadcast_to(grad, (near,) + grad.shape), NEAR, 0, 0)
    grad_down, grad_up = call(
        finish_kernel,
        [shape((3 * RANK, width), F32), shape((3 * RANK, queries.shape[1]), F32)],
        [VMEM],
        1,
    )(grad.reshape(rows, HEAD))
    grad_down = grad_down.reshape(3, RANK, width).transpose(0, 2, 1)
    grad_up = grad_up.reshape(3, RANK, -1)
    return qkv, grad_down, grad_up


def solution(mesh):
    count, columns = mesh.devices.shape
    across = 4 if count >= 128 else 2
    fine = Mesh(mesh.devices.reshape(-1, 2, across, 2, columns), CTX + ("head",))
    in_specs = (
        P(CTX, "head"),
        P(CTX, "head"),
        P(CTX, "head"),
        P(CTX, "head"),
        P(CTX, "head"),
        P(None, "head", None),
        P(None, None, "head"),
        P("head"),
    )
    out_specs = (P(None, CTX, "head"), P(None, "head", None), P(None, None, "head"))
    return jax.shard_map(local, mesh=fine, in_specs=in_specs, out_specs=out_specs, check_vma=False)
```

```python
import functools
import math

import jax
import jax.numpy as jnp
from jax import lax
from jax.experimental import pallas as pl
from jax.experimental.pallas import tpu as pltpu
from jax.sharding import Mesh, PartitionSpec as P

HEAD = 128
RANK = 16
TILE = 256
CTX = ("zh", "zl", "x", "yh")
FAR = "zh"
NEAR = ("zl", "x", "yh")
F32 = jnp.float32
BF16 = jnp.bfloat16
VMEM_BYTES = 48 * 1024 * 1024


def dot_nt(left, right):
    return lax.dot_general(left, right, (((1,), (1,)), ((), ())), preferred_element_type=F32)


def dot_tn(left, right):
    return lax.dot_general(left, right, (((0,), (0,)), ((), ())), preferred_element_type=F32)


def dot_nn(left, right):
    return lax.dot_general(left, right, (((1,), (0,)), ((), ())), preferred_element_type=F32)


def parity_here():
    return lax.axis_index("yh")


def list_heads(flags_ref, order_ref, key, count=0):
    count = jnp.int32(count)
    for head in range(flags_ref.shape[0]):
        chosen = key(flags_ref[head])

        @pl.when(chosen)
        def _():
            order_ref[count] = head

        count = count + chosen.astype(jnp.int32)
    return count


def is_first(flag):
    return ((flag + parity_here()) & 1) == 0


def is_second(flag):
    return ((flag + parity_here()) & 1) == 1


def columns_of(head):
    return pl.ds(pl.multiple_of(head * HEAD, HEAD), HEAD)


def causal_mask(rows, columns):
    keys = lax.broadcasted_iota(jnp.int32, (rows, columns), 0)
    queries = lax.broadcasted_iota(jnp.int32, (rows, columns), 1)
    return keys <= queries


def merge_stats(one, other, factor):
    top = jnp.maximum(one[0], other[0])
    weights = [jnp.exp2((stats[0] - top) * factor) for stats in (one, other)]
    total = one[1] * weights[0] + other[1] * weights[1]
    mixed = one[2] * weights[0] + other[2] * weights[1]
    return top, total, mixed


def low_parts(probs, dprobs, delta):
    return probs.astype(BF16), (probs * (dprobs - delta)).astype(BF16)


def join(function, wide, narrow):
    if wide is None or wide.shape == narrow.shape:
        return narrow if wide is None else function(wide, narrow)
    first = wide.shape[1] - narrow.shape[1]
    return jnp.concatenate([wide[:, :first], function(wide[:, first:], narrow)], 1)


def col_sum(value):
    return jnp.sum(value, axis=0, keepdims=True)


class Head:
    def __init__(self, queries, grads, factor):
        self.queries, self.grads, self.factor = queries, grads, factor

    def full_block(self, pair, own_stats):
        scores = dot_nt(pair[0], self.queries)
        dprobs = dot_nt(pair[1], self.grads)
        own_top = jnp.max(scores, axis=0, keepdims=True)
        exponent = jnp.exp2((scores - own_top) * self.factor)
        stats = own_top, col_sum(exponent), col_sum(exponent * dprobs)
        top, total, mixed = merge_stats(stats, own_stats, self.factor)
        inverse = 1.0 / total
        delta = mixed * inverse
        probs = exponent * (jnp.exp2((own_top - top) * self.factor) * inverse)
        return low_parts(probs, dprobs, delta), (top, inverse, delta)

    def own_products(self, own):
        pieces = []
        for start in range(0, self.queries.shape[0], TILE):
            scores = dot_nt(own[0][start : start + TILE], self.queries[start:])
            scores = jnp.where(causal_mask(*scores.shape), scores, -jnp.inf)
            dprobs = dot_nt(own[1][start : start + TILE], self.grads[start:])
            pieces.append((start, scores, dprobs))
        return pieces

    def own_stats(self, pieces):
        top = total = mixed = None
        for _, scores, _ in pieces:
            top = join(jnp.maximum, top, jnp.max(scores, axis=0, keepdims=True))
        exponents = []
        for start, scores, dprobs in pieces:
            exponents.append(jnp.exp2((scores - top[:, start:]) * self.factor))
            total = join(jnp.add, total, col_sum(exponents[-1]))
            mixed = join(jnp.add, mixed, col_sum(exponents[-1] * dprobs))
        return exponents, (top, total, mixed)

    def own_block(self, own, weights):
        query_t, key_grads, value_grads = None, [], []
        for start, probs, dprobs, delta in weights:
            probs, dscores = low_parts(probs, dprobs, delta)
            query_t = join(jnp.add, query_t, dot_tn(own[0][start : start + TILE], dscores))
            key_grads.append(dot_nn(dscores, self.queries[start:]))
            value_grads.append(dot_nn(probs, self.grads[start:]))
        return query_t, jnp.concatenate(key_grads, 0), jnp.concatenate(value_grads, 0)


def fetch(sides, refs, slot, pair_ref):
    for at, parity, base in sides:
        ref = refs[at]
        here = (slot >= base) & (slot < base + ref.shape[0])
        if parity is not None:
            here = here & (parity_here() == parity)

        @pl.when(here)
        def _():
            pair_ref[...] = ref[slot - base]


def pack_kernel(flags_ref, q_ref, k_ref, v_ref, g_ref, shifted_ref, *refs):
    *out_refs, order_ref = refs
    heads = flags_ref.shape[0]
    total = jnp.int32(0)
    for head in range(heads):
        total = total + flags_ref[head]
    shifted_ref[0] = total
    even = 2 * total == heads
    major = (2 * total > heads).astype(jnp.int32)

    def ahead(flag):
        return jnp.where(even, (flag + parity_here()) & 1, (flag + major) & 1) == 0

    count = list_heads(flags_ref, order_ref, ahead)
    list_heads(flags_ref, order_ref, lambda flag: jnp.logical_not(ahead(flag)), count)
    base = 0
    for out_ref in out_refs:
        for slot in range(out_ref.shape[0]):
            head = order_ref[base + slot]
            cols = columns_of(head)

            def send(a_ref, b_ref):
                out_ref[slot, 0] = a_ref[:, cols]
                out_ref[slot, 1] = b_ref[:, cols]

            first = is_first(flags_ref[head])
            pl.when(first)(functools.partial(send, k_ref, v_ref))
            pl.when(jnp.logical_not(first))(functools.partial(send, q_ref, g_ref))
        base += out_ref.shape[0]


def early_kernel(factor, scale, flags_ref, q_ref, k_ref, v_ref, g_ref, dq_ref, dk_ref, dv_ref, stats_ref, order_ref):
    count = list_heads(flags_ref, order_ref, is_second)

    def rows(slot, _):
        cols = columns_of(order_ref[slot])
        head = Head(q_ref[:, cols], g_ref[:, cols], factor)
        _, stats = head.own_stats(head.own_products((k_ref[:, cols], v_ref[:, cols])))
        for row in range(3):
            stats_ref[slot, row : row + 1] = stats[row]
        return 0

    lax.fori_loop(0, count, rows, 0)
    count = list_heads(flags_ref, order_ref, is_first)

    def step(slot, _):
        cols = columns_of(order_ref[slot])
        own = (k_ref[:, cols], v_ref[:, cols])
        head = Head(q_ref[:, cols], g_ref[:, cols], factor)
        pieces = head.own_products(own)
        exponents, (_, total, mixed) = head.own_stats(pieces)
        inverse = 1.0 / total
        delta = mixed * inverse
        query_t, dk, dv = head.own_block(
            own,
            [
                (start, exponent * inverse[:, start:], dprobs, delta[:, start:])
                for (start, _, dprobs), exponent in zip(pieces, exponents)
            ],
        )
        dq_ref[slot] = (query_t.T * scale).astype(BF16)
        dk_ref[slot] = dk
        dv_ref[slot] = dv
        return 0

    lax.fori_loop(0, count, step, 0)


def head_stats(stats_ref, slot):
    return tuple(stats_ref[slot, row : row + 1] for row in range(3))


def late_kernel(
    factor, scale, kv_sides, qg_sides, flags_ref, q_ref, k_ref, v_ref, g_ref, stats_ref,
    moved_ref, dq_ref, dk_ref, dv_ref, up_ref, *refs
):
    *other_refs, out_ref, back_ref, order_ref, pair_ref = refs
    count = list_heads(flags_ref, order_ref, is_second)

    def second(slot, _):
        fetch(kv_sides, other_refs, slot, pair_ref)
        cols = columns_of(order_ref[slot])
        own = (k_ref[:, cols], v_ref[:, cols])
        before = (pair_ref[0], pair_ref[1])
        head = Head(q_ref[:, cols], g_ref[:, cols], factor)
        (_, dscores), (top, inverse, delta) = head.full_block(before, head_stats(stats_ref, slot))
        query_t, dk, dv = head.own_block(
            own,
            [
                (
                    start,
                    jnp.exp2((scores - top[:, start:]) * factor) * inverse[:, start:],
                    dprobs,
                    delta[:, start:],
                )
                for start, scores, dprobs in head.own_products(own)
            ],
        )
        query_t = query_t + dot_tn(before[0], dscores)
        out_ref[0, :, cols] = (query_t.T * scale).astype(BF16)
        out_ref[1, :, cols] = (dk * scale).astype(BF16)
        out_ref[2, :, cols] = dv.astype(BF16)
        return 0

    lax.fori_loop(0, count, second, 0)
    count = list_heads(flags_ref, order_ref, is_first)

    def first(slot, _):
        fetch(qg_sides, other_refs, slot, pair_ref)
        cols = columns_of(order_ref[slot])
        head = Head(pair_ref[0], pair_ref[1], factor)
        (probs, dscores), _ = head.full_block(
            (k_ref[:, cols], v_ref[:, cols]), head_stats(moved_ref, slot)
        )
        out_ref[0, :, cols] = dq_ref[slot]
        out_ref[1, :, cols] = ((dk_ref[slot] + dot_nn(dscores, head.queries)) * scale).astype(BF16)
        out_ref[2, :, cols] = (dv_ref[slot] + dot_nn(probs, head.grads)).astype(BF16)
        return 0

    lax.fori_loop(0, count, first, 0)
    for index in range(3):
        back_ref[index * RANK : (index + 1) * RANK] = dot_nt(up_ref[index], out_ref[index]).astype(BF16)


def adapter_kernel(norm_factor, parts_ref, inputs_ref, qkv_ref, out_ref):
    summed = functools.reduce(
        jnp.add, [parts_ref[index].astype(F32) for index in range(parts_ref.shape[0])]
    ).astype(BF16)
    rows = 3 * RANK
    down = dot_nn(summed[:rows], inputs_ref[...]) * norm_factor
    up = jnp.concatenate(
        [
            dot_nn(summed[rows + index * RANK : rows + (index + 1) * RANK], qkv_ref[index])
            for index in range(3)
        ],
        0,
    ) * norm_factor
    place = 0
    for total in (down, up):
        for start in range(0, total.shape[1], HEAD):
            out_ref[place : place + rows] = total[:, start : start + HEAD].astype(BF16)
            place += rows


def finish_kernel(sums_ref, *out_refs):
    place = 0
    for out_ref in out_refs:
        for start in range(0, out_ref.shape[1], HEAD):
            rows = out_ref.shape[0]
            out_ref[:, start : start + HEAD] = sums_ref[place : place + rows].astype(F32)
            place += rows


VMEM = pl.BlockSpec(memory_space=pltpu.VMEM)
SMEM = pl.BlockSpec(memory_space=pltpu.SMEM)


def call(kernel, outs, in_specs, flops, heads=0, scratch=()):
    many = isinstance(outs, (list, tuple))
    return pl.pallas_call(
        kernel,
        out_shape=outs,
        in_specs=in_specs,
        out_specs=[VMEM] * len(outs) if many else VMEM,
        scratch_shapes=([pltpu.SMEM((heads,), jnp.int32)] if heads else []) + list(scratch),
        compiler_params=pltpu.CompilerParams(vmem_limit_bytes=VMEM_BYTES),
        cost_estimate=pl.CostEstimate(flops=flops, bytes_accessed=flops >> 8, transcendentals=0),
    )


def shape(dims, dtype):
    return jax.ShapeDtypeStruct(dims, dtype)


def ring(count, parity, step):
    return [(source, (source + step) % count) for source in range(parity, count, 2)]


def attention(shifted, flags, queries, keys, values, grads, inputs, down_t, up, *packs):
    tok_rows = queries.shape[0]
    heads = flags.shape[0]
    slots = max(heads - shifted, shifted)
    major = int(2 * shifted > heads)
    scale = 1.0 / math.sqrt(HEAD)
    factor = scale * math.log2(math.e)
    count = lax.axis_size(CTX)
    behind = ring(count, 0, -1) + ring(count, 1, -1)
    low = shape((slots, tok_rows, HEAD), BF16)
    full = shape((slots, tok_rows, HEAD), F32)
    unit = 2 * tok_rows * tok_rows * HEAD * slots

    arrived, kv_sides, qg_sides = [], [], []
    base = 0
    for at, pack in enumerate(packs):
        later = base >= slots
        if 2 * slots == heads:
            pairs = behind if later else ring(count, 0, 1) + ring(count, 1, 1)
            (qg_sides if later else kv_sides).append((at, None, base - slots * later))
        else:
            flag = major ^ int(later)
            pairs = ring(count, flag, 1) + ring(count, 1 - flag, -1)
            kv_sides.append((at, 1 - flag, base - slots * later))
            qg_sides.append((at, flag, base - slots * later))
        arrived.append(lax.ppermute(pack, CTX, pairs))
        base += pack.shape[0]
    *first, stats = call(
        functools.partial(early_kernel, factor, scale),
        [low, full, full, shape((slots, 8, tok_rows), F32)],
        [SMEM] + [VMEM] * 4,
        1,
        heads,
    )(flags, queries, keys, values, grads)
    stats, moved = lax.optimization_barrier((stats, lax.ppermute(stats, CTX, behind)))
    low_rank = dot_nt(down_t, inputs).astype(BF16)
    qkv, back = call(
        functools.partial(late_kernel, factor, scale, kv_sides, qg_sides),
        [shape((3,) + queries.shape, BF16), shape((3 * RANK, tok_rows), BF16)],
        [SMEM] + [VMEM] * (10 + len(arrived)),
        12 * unit,
        heads,
        [pltpu.VMEM((2, tok_rows, HEAD), BF16)],
    )(flags, queries, keys, values, grads, stats, moved, *first, up, *arrived)
    return qkv, jnp.concatenate([back, low_rank], 0)


def local(inputs, queries, keys, values, grads, down, up, flags):
    tok_rows = queries.shape[0]
    heads = flags.shape[0]
    width = inputs.shape[1]
    seq_total = lax.axis_size(CTX) * tok_rows
    least = (heads + 1) // 2
    sizes = [least] + [1] * (heads - least)
    shifted, *packs = pl.pallas_call(
        pack_kernel,
        out_shape=[shape((1,), jnp.int32)] + [shape((size, 2, tok_rows, HEAD), BF16) for size in sizes],
        in_specs=[SMEM] + [VMEM] * 4,
        out_specs=[SMEM] + [VMEM] * len(sizes),
        scratch_shapes=[pltpu.SMEM((heads,), jnp.int32)],
        compiler_params=pltpu.CompilerParams(vmem_limit_bytes=VMEM_BYTES),
    )(flags, queries, keys, values, grads)
    down_t = down.transpose(0, 2, 1).reshape(3 * RANK, width)
    qkv, parts = lax.switch(
        shifted.reshape(()),
        [functools.partial(attention, number) for number in range(heads + 1)],
        flags, queries, keys, values, grads, inputs, down_t, up, *packs,
    )
    parts = lax.all_gather(parts, "head")
    rows = 3 * RANK * (width + queries.shape[1]) // HEAD
    grad = call(
        functools.partial(adapter_kernel, 1.0 / math.sqrt(seq_total)),
        shape((rows, HEAD), BF16),
        [VMEM] * 3,
        1 << 28,
    )(parts, inputs, qkv)
    near = lax.axis_size(NEAR)
    grad = lax.all_to_all(grad.reshape(near, rows // near, HEAD), NEAR, 0, 0)
    grad = jnp.sum(grad.astype(F32), 0).astype(BF16)
    far = lax.axis_size(FAR)
    grad = lax.all_to_all(jnp.broadcast_to(grad, (far,) + grad.shape), FAR, 0, 0)
    grad = jnp.sum(grad.astype(F32), 0).astype(BF16)
    grad = lax.all_to_all(jnp.broadcast_to(grad, (near,) + grad.shape), NEAR, 0, 0)
    grad_down, grad_up = call(
        finish_kernel,
        [shape((3 * RANK, width), F32), shape((3 * RANK, queries.shape[1]), F32)],
        [VMEM],
        1,
    )(grad.reshape(rows, HEAD))
    grad_down = grad_down.reshape(3, RANK, width).transpose(0, 2, 1)
    grad_up = grad_up.reshape(3, RANK, -1)
    return qkv, grad_down, grad_up


def solution(mesh):
    count, columns = mesh.devices.shape
    across = 4 if count >= 128 else 2
    fine = Mesh(mesh.devices.reshape(-1, 2, across, 2, columns), CTX + ("head",))
    in_specs = (
        P(CTX, "head"),
        P(CTX, "head"),
        P(CTX, "head"),
        P(CTX, "head"),
        P(CTX, "head"),
        P(None, "head", None),
        P(None, None, "head"),
        P("head"),
    )
    out_specs = (P(None, CTX, "head"), P(None, "head", None), P(None, None, "head"))
    return jax.shard_map(local, mesh=fine, in_specs=in_specs, out_specs=out_specs, check_vma=False)
```

```python
import functools
import math

import jax
import jax.numpy as jnp
from jax import lax
from jax.experimental import pallas as pl
from jax.experimental.pallas import tpu as pltpu
from jax.sharding import Mesh, PartitionSpec as P

HEAD = 128
RANK = 16
TILE = 256
CTX = ("zh", "zl", "x", "yh")
FAR = "zh"
NEAR = ("zl", "x", "yh")
F32 = jnp.float32
BF16 = jnp.bfloat16
VMEM_BYTES = 48 * 1024 * 1024


def dot_nt(left, right):
    return lax.dot_general(left, right, (((1,), (1,)), ((), ())), preferred_element_type=F32)


def dot_tn(left, right):
    return lax.dot_general(left, right, (((0,), (0,)), ((), ())), preferred_element_type=F32)


def dot_nn(left, right):
    return lax.dot_general(left, right, (((1,), (0,)), ((), ())), preferred_element_type=F32)


def parity_here():
    return lax.axis_index("yh")


def list_heads(flags_ref, order_ref, key, count=0):
    count = jnp.int32(count)
    for head in range(flags_ref.shape[0]):
        chosen = key(flags_ref[head])

        @pl.when(chosen)
        def _():
            order_ref[count] = head

        count = count + chosen.astype(jnp.int32)
    return count


def is_first(flag):
    return ((flag + parity_here()) & 1) == 0


def is_second(flag):
    return ((flag + parity_here()) & 1) == 1


def columns_of(head):
    return pl.ds(pl.multiple_of(head * HEAD, HEAD), HEAD)


def causal_mask(rows, columns):
    keys = lax.broadcasted_iota(jnp.int32, (rows, columns), 0)
    queries = lax.broadcasted_iota(jnp.int32, (rows, columns), 1)
    return keys <= queries


def merge_stats(one, other, factor):
    top = jnp.maximum(one[0], other[0])
    weights = [jnp.exp2((stats[0] - top) * factor) for stats in (one, other)]
    total = one[1] * weights[0] + other[1] * weights[1]
    mixed = one[2] * weights[0] + other[2] * weights[1]
    return top, total, mixed


def low_parts(probs, dprobs, delta):
    return probs.astype(BF16), (probs * (dprobs - delta)).astype(BF16)


def join(function, wide, narrow):
    if wide is None or wide.shape == narrow.shape:
        return narrow if wide is None else function(wide, narrow)
    first = wide.shape[1] - narrow.shape[1]
    return jnp.concatenate([wide[:, :first], function(wide[:, first:], narrow)], 1)


def col_sum(value):
    return jnp.sum(value, axis=0, keepdims=True)


class Head:
    def __init__(self, queries, grads, factor):
        self.queries, self.grads, self.factor = queries, grads, factor

    def full_block(self, pair, own_stats):
        scores = dot_nt(pair[0], self.queries)
        dprobs = dot_nt(pair[1], self.grads)
        own_top = jnp.max(scores, axis=0, keepdims=True)
        exponent = jnp.exp2((scores - own_top) * self.factor)
        stats = own_top, col_sum(exponent), col_sum(exponent * dprobs)
        top, total, mixed = merge_stats(stats, own_stats, self.factor)
        inverse = 1.0 / total
        delta = mixed * inverse
        probs = exponent * (jnp.exp2((own_top - top) * self.factor) * inverse)
        return low_parts(probs, dprobs, delta), (top, inverse, delta)

    def own_products(self, own):
        pieces = []
        for start in range(0, self.queries.shape[0], TILE):
            scores = dot_nt(own[0][start : start + TILE], self.queries[start:])
            scores = jnp.where(causal_mask(*scores.shape), scores, -jnp.inf)
            dprobs = dot_nt(own[1][start : start + TILE], self.grads[start:])
            pieces.append((start, scores, dprobs))
        return pieces

    def own_stats(self, pieces):
        top = total = mixed = None
        for _, scores, _ in pieces:
            top = join(jnp.maximum, top, jnp.max(scores, axis=0, keepdims=True))
        exponents = []
        for start, scores, dprobs in pieces:
            exponents.append(jnp.exp2((scores - top[:, start:]) * self.factor))
            total = join(jnp.add, total, col_sum(exponents[-1]))
            mixed = join(jnp.add, mixed, col_sum(exponents[-1] * dprobs))
        return exponents, (top, total, mixed)

    def own_block(self, own, weights):
        query_t, key_grads, value_grads = None, [], []
        for start, probs, dprobs, delta in weights:
            probs, dscores = low_parts(probs, dprobs, delta)
            query_t = join(jnp.add, query_t, dot_tn(own[0][start : start + TILE], dscores))
            key_grads.append(dot_nn(dscores, self.queries[start:]))
            value_grads.append(dot_nn(probs, self.grads[start:]))
        return query_t, jnp.concatenate(key_grads, 0), jnp.concatenate(value_grads, 0)


def fetch(sides, refs, slot, pair_ref):
    for at, parity, base in sides:
        ref = refs[at]
        here = (slot >= base) & (slot < base + ref.shape[0])
        if parity is not None:
            here = here & (parity_here() == parity)

        @pl.when(here)
        def _():
            pair_ref[...] = ref[slot - base]


def pack_kernel(flags_ref, q_ref, k_ref, v_ref, g_ref, shifted_ref, *refs):
    *out_refs, order_ref, sems = refs
    heads = flags_ref.shape[0]
    total = jnp.int32(0)
    for head in range(heads):
        total = total + flags_ref[head]
    shifted_ref[0] = total
    even = 2 * total == heads
    major = (2 * total > heads).astype(jnp.int32)

    def ahead(flag):
        return jnp.where(even, (flag + parity_here()) & 1, (flag + major) & 1) == 0

    count = list_heads(flags_ref, order_ref, ahead)
    list_heads(flags_ref, order_ref, lambda flag: jnp.logical_not(ahead(flag)), count)
    for act in ("start", "wait"):
        base = 0
        for out_ref in out_refs:
            for slot in range(out_ref.shape[0]):
                head = order_ref[base + slot]
                cols = columns_of(head)

                def send(*pair):
                    for index in range(2):
                        copy = pltpu.make_async_copy(
                            pair[index].at[:, cols], out_ref.at[slot, index], sems.at[base + slot, index]
                        )
                        getattr(copy, act)()

                first = is_first(flags_ref[head])
                pl.when(first)(functools.partial(send, k_ref, v_ref))
                pl.when(jnp.logical_not(first))(functools.partial(send, q_ref, g_ref))
            base += out_ref.shape[0]


def early_kernel(factor, scale, flags_ref, q_ref, k_ref, v_ref, g_ref, dq_ref, dk_ref, dv_ref, stats_ref, order_ref):
    count = list_heads(flags_ref, order_ref, is_second)

    def rows(slot, _):
        cols = columns_of(order_ref[slot])
        head = Head(q_ref[:, cols], g_ref[:, cols], factor)
        _, stats = head.own_stats(head.own_products((k_ref[:, cols], v_ref[:, cols])))
        for row in range(3):
            stats_ref[slot, row : row + 1] = stats[row]
        return 0

    lax.fori_loop(0, count, rows, 0)
    count = list_heads(flags_ref, order_ref, is_first)

    def step(slot, _):
        cols = columns_of(order_ref[slot])
        own = (k_ref[:, cols], v_ref[:, cols])
        head = Head(q_ref[:, cols], g_ref[:, cols], factor)
        pieces = head.own_products(own)
        exponents, (_, total, mixed) = head.own_stats(pieces)
        inverse = 1.0 / total
        delta = mixed * inverse
        query_t, dk, dv = head.own_block(
            own,
            [
                (start, exponent * inverse[:, start:], dprobs, delta[:, start:])
                for (start, _, dprobs), exponent in zip(pieces, exponents)
            ],
        )
        dq_ref[slot] = (query_t.T * scale).astype(BF16)
        dk_ref[slot] = dk
        dv_ref[slot] = dv
        return 0

    lax.fori_loop(0, count, step, 0)


def head_stats(stats_ref, slot):
    return tuple(stats_ref[slot, row : row + 1] for row in range(3))


def late_kernel(
    factor, scale, kv_sides, qg_sides, flags_ref, q_ref, k_ref, v_ref, g_ref, stats_ref,
    moved_ref, dq_ref, dk_ref, dv_ref, up_ref, *refs
):
    *other_refs, out_ref, back_ref, order_ref, pair_ref = refs
    count = list_heads(flags_ref, order_ref, is_second)

    def second(slot, _):
        fetch(kv_sides, other_refs, slot, pair_ref)
        cols = columns_of(order_ref[slot])
        own = (k_ref[:, cols], v_ref[:, cols])
        before = (pair_ref[0], pair_ref[1])
        head = Head(q_ref[:, cols], g_ref[:, cols], factor)
        (_, dscores), (top, inverse, delta) = head.full_block(before, head_stats(stats_ref, slot))
        query_t, dk, dv = head.own_block(
            own,
            [
                (
                    start,
                    jnp.exp2((scores - top[:, start:]) * factor) * inverse[:, start:],
                    dprobs,
                    delta[:, start:],
                )
                for start, scores, dprobs in head.own_products(own)
            ],
        )
        query_t = query_t + dot_tn(before[0], dscores)
        out_ref[0, :, cols] = (query_t.T * scale).astype(BF16)
        out_ref[1, :, cols] = (dk * scale).astype(BF16)
        out_ref[2, :, cols] = dv.astype(BF16)
        return 0

    lax.fori_loop(0, count, second, 0)
    count = list_heads(flags_ref, order_ref, is_first)

    def first(slot, _):
        fetch(qg_sides, other_refs, slot, pair_ref)
        cols = columns_of(order_ref[slot])
        head = Head(pair_ref[0], pair_ref[1], factor)
        (probs, dscores), _ = head.full_block(
            (k_ref[:, cols], v_ref[:, cols]), head_stats(moved_ref, slot)
        )
        out_ref[0, :, cols] = dq_ref[slot]
        out_ref[1, :, cols] = ((dk_ref[slot] + dot_nn(dscores, head.queries)) * scale).astype(BF16)
        out_ref[2, :, cols] = (dv_ref[slot] + dot_nn(probs, head.grads)).astype(BF16)
        return 0

    lax.fori_loop(0, count, first, 0)
    for index in range(3):
        back_ref[index * RANK : (index + 1) * RANK] = dot_nt(up_ref[index], out_ref[index]).astype(BF16)


def adapter_kernel(norm_factor, parts_ref, inputs_ref, qkv_ref, out_ref):
    summed = functools.reduce(
        jnp.add, [parts_ref[index].astype(F32) for index in range(parts_ref.shape[0])]
    ).astype(BF16)
    rows = 3 * RANK
    down = dot_nn(summed[:rows], inputs_ref[...]) * norm_factor
    up = jnp.concatenate(
        [
            dot_nn(summed[rows + index * RANK : rows + (index + 1) * RANK], qkv_ref[index])
            for index in range(3)
        ],
        0,
    ) * norm_factor
    place = 0
    for total in (down, up):
        for start in range(0, total.shape[1], HEAD):
            out_ref[place : place + rows] = total[:, start : start + HEAD].astype(BF16)
            place += rows


def finish_kernel(sums_ref, *out_refs):
    place = 0
    for out_ref in out_refs:
        for start in range(0, out_ref.shape[1], HEAD):
            rows = out_ref.shape[0]
            out_ref[:, start : start + HEAD] = sums_ref[place : place + rows].astype(F32)
            place += rows


VMEM = pl.BlockSpec(memory_space=pltpu.VMEM)
SMEM = pl.BlockSpec(memory_space=pltpu.SMEM)


def call(kernel, outs, in_specs, flops, heads=0, scratch=()):
    many = isinstance(outs, (list, tuple))
    return pl.pallas_call(
        kernel,
        out_shape=outs,
        in_specs=in_specs,
        out_specs=[VMEM] * len(outs) if many else VMEM,
        scratch_shapes=([pltpu.SMEM((heads,), jnp.int32)] if heads else []) + list(scratch),
        compiler_params=pltpu.CompilerParams(vmem_limit_bytes=VMEM_BYTES),
        cost_estimate=pl.CostEstimate(flops=flops, bytes_accessed=flops >> 8, transcendentals=0),
    )


def shape(dims, dtype):
    return jax.ShapeDtypeStruct(dims, dtype)


def ring(count, parity, step):
    return [(source, (source + step) % count) for source in range(parity, count, 2)]


def attention(shifted, flags, queries, keys, values, grads, inputs, down_t, up, *packs):
    tok_rows = queries.shape[0]
    heads = flags.shape[0]
    slots = max(heads - shifted, shifted)
    major = int(2 * shifted > heads)
    scale = 1.0 / math.sqrt(HEAD)
    factor = scale * math.log2(math.e)
    count = lax.axis_size(CTX)
    behind = ring(count, 0, -1) + ring(count, 1, -1)
    low = shape((slots, tok_rows, HEAD), BF16)
    full = shape((slots, tok_rows, HEAD), F32)
    unit = 2 * tok_rows * tok_rows * HEAD * slots

    arrived, kv_sides, qg_sides = [], [], []
    base = 0
    for at, pack in enumerate(packs):
        later = base >= slots
        if 2 * slots == heads:
            pairs = behind if later else ring(count, 0, 1) + ring(count, 1, 1)
            (qg_sides if later else kv_sides).append((at, None, base - slots * later))
        else:
            flag = major ^ int(later)
            pairs = ring(count, flag, 1) + ring(count, 1 - flag, -1)
            kv_sides.append((at, 1 - flag, base - slots * later))
            qg_sides.append((at, flag, base - slots * later))
        arrived.append(lax.ppermute(pack, CTX, pairs))
        base += pack.shape[0]
    *first, stats = call(
        functools.partial(early_kernel, factor, scale),
        [low, full, full, shape((slots, 8, tok_rows), F32)],
        [SMEM] + [VMEM] * 4,
        1,
        heads,
    )(flags, queries, keys, values, grads)
    stats, moved = lax.optimization_barrier((stats, lax.ppermute(stats, CTX, behind)))
    low_rank = dot_nt(down_t, inputs).astype(BF16)
    qkv, back = call(
        functools.partial(late_kernel, factor, scale, kv_sides, qg_sides),
        [shape((3,) + queries.shape, BF16), shape((3 * RANK, tok_rows), BF16)],
        [SMEM] + [VMEM] * (10 + len(arrived)),
        12 * unit,
        heads,
        [pltpu.VMEM((2, tok_rows, HEAD), BF16)],
    )(flags, queries, keys, values, grads, stats, moved, *first, up, *arrived)
    return qkv, jnp.concatenate([back, low_rank], 0)


def local(inputs, queries, keys, values, grads, down, up, flags):
    tok_rows = queries.shape[0]
    heads = flags.shape[0]
    width = inputs.shape[1]
    seq_total = lax.axis_size(CTX) * tok_rows
    least = (heads + 1) // 2
    sizes = [least] + [1] * (heads - least)
    shifted, *packs = pl.pallas_call(
        pack_kernel,
        out_shape=[shape((1,), jnp.int32)] + [shape((size, 2, tok_rows, HEAD), BF16) for size in sizes],
        in_specs=[SMEM] + [pl.BlockSpec(memory_space=pl.ANY)] * 4,
        out_specs=[SMEM] + [VMEM] * len(sizes),
        scratch_shapes=[pltpu.SMEM((heads,), jnp.int32), pltpu.SemaphoreType.DMA((heads, 2))],
        compiler_params=pltpu.CompilerParams(vmem_limit_bytes=VMEM_BYTES),
    )(flags, queries, keys, values, grads)
    down_t = down.transpose(0, 2, 1).reshape(3 * RANK, width)
    qkv, parts = lax.switch(
        shifted.reshape(()),
        [functools.partial(attention, number) for number in range(heads + 1)],
        flags, queries, keys, values, grads, inputs, down_t, up, *packs,
    )
    parts = lax.all_gather(parts, "head")
    rows = 3 * RANK * (width + queries.shape[1]) // HEAD
    grad = call(
        functools.partial(adapter_kernel, 1.0 / math.sqrt(seq_total)),
        shape((rows, HEAD), BF16),
        [VMEM] * 3,
        1 << 28,
    )(parts, inputs, qkv)
    near = lax.axis_size(NEAR)
    grad = lax.all_to_all(grad.reshape(near, rows // near, HEAD), NEAR, 0, 0)
    grad = jnp.sum(grad.astype(F32), 0).astype(BF16)
    far = lax.axis_size(FAR)
    grad = lax.all_to_all(jnp.broadcast_to(grad, (far,) + grad.shape), FAR, 0, 0)
    grad = jnp.sum(grad.astype(F32), 0).astype(BF16)
    grad = lax.all_to_all(jnp.broadcast_to(grad, (near,) + grad.shape), NEAR, 0, 0)
    grad_down, grad_up = call(
        finish_kernel,
        [shape((3 * RANK, width), F32), shape((3 * RANK, queries.shape[1]), F32)],
        [VMEM],
        1,
    )(grad.reshape(rows, HEAD))
    grad_down = grad_down.reshape(3, RANK, width).transpose(0, 2, 1)
    grad_up = grad_up.reshape(3, RANK, -1)
    return qkv, grad_down, grad_up


def solution(mesh):
    count, columns = mesh.devices.shape
    across = 4 if count >= 128 else 2
    fine = Mesh(mesh.devices.reshape(-1, 2, across, 2, columns), CTX + ("head",))
    in_specs = (
        P(CTX, "head"),
        P(CTX, "head"),
        P(CTX, "head"),
        P(CTX, "head"),
        P(CTX, "head"),
        P(None, "head", None),
        P(None, None, "head"),
        P("head"),
    )
    out_specs = (P(None, CTX, "head"), P(None, "head", None), P(None, None, "head"))
    return jax.shard_map(local, mesh=fine, in_specs=in_specs, out_specs=out_specs, check_vma=False)
```
